512 devices in a mesh: grp: 8 (over z_lo, core), box: 64 (over z_hi, x, y).
Axes of the slice: x: 4, y: 8, z: 8 (z_hi: 2, z_lo: 4; z = z_hi * 4 + z_lo), core: 2. Of those that a mesh axis runs over, the one named last changes fastest.
Arguments:
- coarse_dens: float32 [728, 512], P(None, ('grp', 'box')), may hold values from -6 to 6
- owner_slot: int32 [512], replicated, may hold values from 0 to 511, as said below
- check_to_equiv: float32 [728, 728], replicated, may hold values from -0.21875 to 0.21875
- parent_own: float32 [728, 4096], P(None, ('grp', 'box')), may hold values from -6 to 6
- leaf_own: float32 [728, 32768], P(None, ('grp', 'box')), may hold values from -6 to 6
- leaf_counts: int32 [512, 64], P(('grp', 'box')), may hold values from 1 to 128, 2048 in all within a row
- particles: float32 [3, 1048576], P(None, ('grp', 'box')), may hold values from -0.9 to 0.9
- panels: float32 [4, 524288], P(None, ('grp', 'box')), as said below
- near_part: int32 [32768], P(('grp', 'box')), may hold values from 0 to 15
- near_pan: int32 [32768], P(('grp', 'box')), may hold values from 0 to 23
- near_count: int32 [512], P(('grp', 'box')), may hold values from 8 to 64, as said below
Outputs:
- field_grad: float32 [4, 1048576], P(None, ('grp', 'box'))
The draws below stay inside these ranges and needn't reach their ends.
Inputs may be any that keep to these rules, and one draw needn't show every extreme that they name: `owner_slot`: a permutation that keeps coarse box k among the 64 slots of group k // 64. `near_count`: some device has all 64 slots live. `panels`: rows 0 to 2 hold a panel centre within 1 in each coordinate of the centre of some leaf of the device that holds the panel; row 3 holds its strength.
All inputs are finite; a program needn't handle non-finite values.
Results may differ from the reference program's by a relative error of at most 0.0003.
Values sent between devices are 32-bit elements; how exact they have to be, the bound alone decides.
A program may use at most 64 MiB of HBM per device.

```python
import math
from functools import partial
import jax
import jax.numpy as jnp
import numpy as np
from jax import lax

ORDER = 12
P_SIZE = 728
LEAF_DEV = 64
PART_DEV = 2048
PAN_DEV = 1024
TILE_CAP = 64
NLEAVES = 32768
NPARENTS = 4096
NCOARSE = 512
GRP_SLOTS = 64
NPART = 1048576
NPANELS = 524288
NTILES = 32768
DEVICES = 512


def leaf_centres_drawn(leaf_index):
    coords = []
    for axis_bit in range(3):
        coord_val = jnp.zeros_like(leaf_index)
        for bit_level in range(10):
            bit_value = jnp.bitwise_and(jnp.right_shift(leaf_index, 3 * bit_level + axis_bit), 1)
            coord_val = coord_val + jnp.left_shift(bit_value, bit_level)
        coords.append(2 * coord_val + 1)
    return jnp.stack(coords, 0).astype(jnp.float32)


def draw_owner_slot(key, part):
    group_keys = jax.random.split(key, NCOARSE // GRP_SLOTS)

    def one_group(group_key):
        return jax.random.permutation(group_key, GRP_SLOTS)
    shuffled = jax.vmap(one_group)(group_keys)
    base = (jnp.arange(NCOARSE // GRP_SLOTS) * GRP_SLOTS)[:, None]
    return (shuffled + base).reshape(-1).astype(jnp.int32)


def draw_near_count(key, part):
    first_key, second_key = jax.random.split(key)
    counts = jax.random.randint(first_key, (DEVICES,), TILE_CAP // 8, TILE_CAP + 1)
    fullest = jax.random.randint(second_key, (), 0, DEVICES)
    return jnp.where(jnp.arange(DEVICES) == fullest, TILE_CAP, counts).astype(jnp.int32)


def draw_panels(key, part):
    leaf_key, place_key, charge_key = jax.random.split(key, 3)
    panel_dev = jnp.arange(NPANELS) // PAN_DEV
    leaf_pick = (jax.random.randint(leaf_key, (NPANELS,), 0, LEAF_DEV) + panel_dev * LEAF_DEV).astype(jnp.int32)
    offsets = jax.random.uniform(place_key, (3, NPANELS), jnp.float32, -1.0, 1.0)
    places = leaf_centres_drawn(leaf_pick) + offsets
    strength = jax.random.normal(charge_key, (NPANELS,), jnp.float32)
    strength = jnp.clip(strength, -4.0, 4.0)
    return jnp.concatenate([places, strength[None]], 0).astype(jnp.float32)


def touch_ends(result, own_key, smallest, largest):
    longest = result.shape.index(max(result.shape))
    spots = []
    for shift in (0, 1):
        where = [jax.random.randint(jax.random.fold_in(own_key, axis), (), 0, length) for axis, length in enumerate(result.shape)]
        where[longest] = (where[longest] + shift) % result.shape[longest]
        spots.append(tuple(where))
    return result.at[spots[0]].set(smallest).at[spots[1]].set(largest)


def block_levels(stream_key, shape, cuts, smallest, high):
    def one(position, shards_of):
        steps = jax.random.uniform(jax.random.fold_in(jax.random.fold_in(stream_key, 6), position), (shards_of,), jnp.float32, smallest / len(cuts), high / len(cuts))
        return jnp.repeat(jnp.exp(steps), shape[position] // shards_of).reshape((-1,) + (1,) * (len(shape) - position - 1))

    gain = one(*cuts[0])
    for cut in cuts[1:]:
        gain = gain * one(*cut)
    return gain


def profile(count, total, bound, lean):
    portions = [(1 << 20) // math.isqrt(standing ** lean) + 1 for standing in range(2, count + 1)]
    rest, given = total - bound - (count - 1), [1] * (count - 1)
    while rest > 0:
        candidates = [i for i in range(count - 1) if given[i] < bound]
        mass, remaining = sum([portions[i] for i in candidates]), rest
        for i in candidates:
            extra = min(bound - given[i], max(1, remaining * portions[i] // mass), rest)
            given[i] = given[i] + extra
            rest = rest - extra
    return np.array([bound] + given)


def uneven(stream_key, amount, total, limit, lean):
    if amount == 2:
        one = jax.random.randint(stream_key, (), max(1, total - limit), min(limit, total - 1) + 1)
        return jnp.stack([one, total - one])
    tallies = jnp.asarray(profile(amount, total, limit, lean), jnp.int32)
    twos = (amount - 1) // 2
    donor, sink = tallies[1:1 + 2 * twos:2], tallies[2:2 + 2 * twos:2]
    margin = jnp.minimum(donor - 1, limit - sink)
    passed = jax.random.randint(jax.random.fold_in(stream_key, 1), (twos,), 0, 1 << 20) % (margin + 1)
    tallies = tallies.at[1:1 + 2 * twos:2].set(donor - passed).at[2:2 + 2 * twos:2].set(sink + passed)
    return tallies[jax.random.permutation(jax.random.fold_in(stream_key, 2), amount)]


def gaussian(stream_key, extent, scale, limit, cuts=(), dtype=jnp.bfloat16):
    loudness = block_levels(stream_key, extent, cuts, -0.22, 0.18) if cuts else 1.0
    values = jax.random.normal(stream_key, extent, jnp.float32) * scale * loudness
    return jnp.minimum(jnp.maximum(values, -limit), limit).astype(dtype)


def setup_inputs(seed: int = 0) -> dict:
    key_of = jax.random.split(jax.random.key(seed), 12)
    coarse_dens = gaussian(key_of[0], (P_SIZE, NCOARSE), 1.0, 6.0, ((1, 512),), jnp.float32)
    owner_slot = draw_owner_slot(jax.random.fold_in(key_of[11], 71), 0)
    check_to_equiv = gaussian(key_of[2], (P_SIZE, P_SIZE), P_SIZE ** -0.5, 0.21875, (), jnp.float32)
    parent_own = gaussian(key_of[3], (P_SIZE, NPARENTS), 1.0, 6.0, ((1, 512),), jnp.float32)
    leaf_own = gaussian(key_of[4], (P_SIZE, NLEAVES), 1.0, 6.0, ((1, 512),), jnp.float32)
    leaf_counts = jax.vmap(lambda own: uneven(own, LEAF_DEV, PART_DEV, 4 * PART_DEV // LEAF_DEV, 2))(jax.random.split(key_of[5], DEVICES)).reshape((DEVICES, LEAF_DEV)).astype(jnp.int32)
    particles = jnp.clip(jax.random.uniform(key_of[6], (3, NPART), jnp.float32, -0.9, 0.9) * block_levels(key_of[6], (3, NPART), ((1, 512),), -0.4, 0.0), -0.9, 0.9)
    panels = draw_panels(jax.random.fold_in(key_of[11], 71), 0)
    near_part = touch_ends(jax.random.randint(key_of[8], (NTILES,), 0, PART_DEV // 128), jax.random.fold_in(key_of[8], 1), 0, (PART_DEV // 128) - 1).astype(jnp.int32)
    near_pan = touch_ends(jax.random.randint(key_of[9], (NTILES,), 0, 3 * PAN_DEV // 128), jax.random.fold_in(key_of[9], 1), 0, (3 * PAN_DEV // 128) - 1).astype(jnp.int32)
    near_count = draw_near_count(jax.random.fold_in(key_of[11], 71), 0)
    return {"coarse_dens": coarse_dens, "owner_slot": owner_slot, "check_to_equiv": check_to_equiv, "parent_own": parent_own, "leaf_own": leaf_own, "leaf_counts": leaf_counts, "particles": particles, "panels": panels, "near_part": near_part, "near_pan": near_pan, "near_count": near_count}


EQUIV_RADIUS = 2.95
CHECK_RADIUS = 1.05
SOFTEN_SQ = 0.0625
FOUR_PI = 4.0 * math.pi

def surface_points(edge_points):
    spacing = np.linspace(-1.0, 1.0, edge_points)
    lattice = np.stack(np.meshgrid(spacing, spacing, spacing, indexing='ij'), 0).reshape(3, -1)
    on_surface = np.max(np.abs(lattice), axis=0) > 0.999
    return lattice[:, on_surface].astype(np.float32)

def leaf_centres(leaf_index):
    coords = []
    for axis_bit in range(3):
        coord_val = jnp.zeros_like(leaf_index)
        for bit_level in range(10):
            bit_value = jnp.bitwise_and(jnp.right_shift(leaf_index, 3 * bit_level + axis_bit), 1)
            coord_val = coord_val + jnp.left_shift(bit_value, bit_level)
        coords.append(2 * coord_val + 1)
    return jnp.stack(coords, 0).astype(jnp.float32)

def transfer_kernel(octant, points):
    corner = np.array([octant & 1, octant >> 1 & 1, octant >> 2 & 1], np.float32) - 0.5
    targets = jnp.asarray(corner)[:, None] + 0.5 * CHECK_RADIUS * points
    sources = EQUIV_RADIUS * points
    separation = targets[:, :, None] - sources[:, None, :]
    return lax.rsqrt(lax.optimization_barrier(jnp.sum(separation * separation, 0))) / FOUR_PI

def descend(upper, check_to_equiv, own_terms, points):
    checks = [jnp.dot(transfer_kernel(octant, points), upper, precision=lax.Precision.HIGHEST, preferred_element_type=jnp.float32) for octant in range(8)]
    stacked = jnp.stack(checks, 2).reshape(upper.shape[0], upper.shape[1] * 8)
    return jnp.dot(check_to_equiv, stacked, precision=lax.Precision.HIGHEST, preferred_element_type=jnp.float32) + own_terms

def far_field(density, local_pos, points):
    sources = EQUIV_RADIUS * points
    separation = local_pos[:, None, :] - sources[:, :, None]
    inverse = lax.rsqrt(lax.optimization_barrier(jnp.sum(separation * separation, 0)))
    weighted = density * inverse / FOUR_PI
    potential = lax.optimization_barrier(jnp.sum(weighted, 0))
    gradient = -lax.optimization_barrier(jnp.sum(separation * (weighted * inverse * inverse)[None], 1))
    return jnp.concatenate([potential[None], gradient], 0)

def near_tile(part_pos, panel_tile):
    separation = part_pos[:, :, None] - panel_tile[:3, None, :]
    inverse = lax.rsqrt(lax.optimization_barrier(jnp.sum(separation * separation, 0)) + SOFTEN_SQ)
    weighted = panel_tile[3][None, :] * inverse / FOUR_PI
    potential = lax.optimization_barrier(jnp.sum(weighted, 1))
    gradient = -lax.optimization_barrier(jnp.sum(separation * (weighted * inverse * inverse)[None], 2))
    return jnp.concatenate([potential[None], gradient], 0)

def reference(coarse_dens, owner_slot, check_to_equiv, parent_own, leaf_own, leaf_counts, particles, panels, near_part, near_pan, near_count):
    points = jnp.asarray(surface_points(ORDER))
    coarse = jnp.take(coarse_dens, owner_slot, axis=1)
    parents = descend(coarse, check_to_equiv, parent_own, points)
    leaves = descend(parents, check_to_equiv, leaf_own, points)
    running = jnp.cumsum(leaf_counts, axis=1)
    part_index = jnp.arange(PART_DEV).astype(jnp.int32)
    leaf_local = jax.vmap(partial(jnp.searchsorted, side='right'), in_axes=(0, None))(running, part_index)
    global_leaf = (jnp.arange(DEVICES)[:, None] * LEAF_DEV + leaf_local).reshape(-1).astype(jnp.int32)
    centres = leaf_centres(jnp.arange(NLEAVES).astype(jnp.int32))
    positions = particles + jnp.take(centres, global_leaf, axis=1)
    block_len = 4096 if NPART % 4096 == 0 else 256

    def far_block(first_row):
        leaf_ids = lax.dynamic_slice_in_dim(global_leaf, first_row, block_len)
        local_pos = lax.dynamic_slice_in_dim(particles, first_row, block_len, 1)
        return far_field(jnp.take(leaves, leaf_ids, axis=1), local_pos, points)
    firsts = (jnp.arange(NPART // block_len) * block_len).astype(jnp.int32)
    distant = lax.map(far_block, firsts).transpose(1, 0, 2).reshape(4, NPART)
    slot_index = jnp.arange(NTILES).astype(jnp.int32)
    tile_dev = slot_index // TILE_CAP
    active = (slot_index % TILE_CAP < near_count[tile_dev]).astype(jnp.float32)
    part_start = ((tile_dev * (PART_DEV // 128) + near_part) * 128).astype(jnp.int32)
    panel_start = (tile_dev * PAN_DEV + near_pan * 128).astype(jnp.int32)
    padded = jnp.pad(panels, ((0, 0), (PAN_DEV, PAN_DEV)))

    def one_tile(part_first, panel_first):
        return near_tile(lax.dynamic_slice_in_dim(positions, part_first, 128, 1), lax.dynamic_slice_in_dim(padded, panel_first, 128, 1))

    def near_group(first_row):
        part_firsts = lax.dynamic_slice_in_dim(part_start, first_row, 128)
        panel_firsts = lax.dynamic_slice_in_dim(panel_start, first_row, 128)
        return jax.vmap(one_tile)(part_firsts, panel_firsts)
    groups = (jnp.arange(NTILES // 128) * 128).astype(jnp.int32)
    contribs = lax.map(near_group, groups).reshape(NTILES, 4, 128) * active[:, None, None]
    targets = (part_start[:, None] + jnp.arange(128)[None, :]).reshape(-1).astype(jnp.int32)
    nearby = jnp.zeros((4, NPART), jnp.float32).at[:, targets].add(contribs.transpose(1, 0, 2).reshape(4, -1))
    return distant + nearby
```

```python
import functools
import math

import jax
import jax.numpy as jnp
import ml_dtypes
import numpy as np
from jax import lax
from jax.experimental import pallas as pl
from jax.experimental.pallas import tpu as pltpu
from jax.sharding import PartitionSpec as P

ORDER = 12
EQUIV_RADIUS = 2.95
CHECK_RADIUS = 1.05
SOFTEN_SQ = 0.0625
FOUR_PI = 4.0 * math.pi
MESH = pl.DeviceIdType.MESH

NPTS = 728
MAGS = 91
BLK = 96
WID = 8 * BLK
F32, BF16 = jnp.float32, jnp.bfloat16


def surface_points(edge_points):
    spacing = np.linspace(-1.0, 1.0, edge_points)
    lattice = np.stack(np.meshgrid(spacing, spacing, spacing, indexing="ij"), 0).reshape(3, -1)
    on_surface = np.max(np.abs(lattice), axis=0) > 0.999
    return lattice[:, on_surface].astype(np.float32)


def split2(value):
    hi = value.astype(ml_dtypes.bfloat16)
    lo = (value - hi.astype(np.float32)).astype(ml_dtypes.bfloat16)
    return hi, lo


@functools.lru_cache(maxsize=None)
def tables():
    points = surface_points(ORDER).astype(np.float64)
    grid = np.rint((points + 1.0) * (ORDER - 1) / 2.0).astype(int)
    index = {tuple(g): i for i, g in enumerate(grid.T)}
    half = ORDER // 2
    mags = [g for g in grid.T if min(g) >= half]
    order = np.full(WID, -1)
    for s in range(8):
        for m, g in enumerate(mags):
            key = tuple(g[a] if s >> a & 1 else ORDER - 1 - g[a] for a in range(3))
            order[BLK * s + m] = index[key]
    live = order >= 0
    placed = points[:, np.where(live, order, 0)]
    targets = -0.5 + 0.5 * CHECK_RADIUS * placed
    separation = targets[:, :, None] - EQUIV_RADIUS * placed[:, None, :]
    k0 = 1.0 / (FOUR_PI * np.sqrt(np.sum(separation * separation, 0)))
    k0 = np.where(live[:, None] & live[None, :], k0, 0.0).astype(np.float32)
    k_pair = np.concatenate(split2(k0), 1)
    perm = np.zeros((WID, WID), np.float32)
    perm[np.nonzero(live)[0], order[live]] = 1.0
    size = np.ones((3, BLK))
    size[:, :MAGS] = np.array([[points[a, index[tuple(g)]] for g in mags] for a in range(3)])
    rows = np.concatenate([2.0 * EQUIV_RADIUS * size, EQUIV_RADIUS**2 * np.sum(size * size, 0)[None]], 0)
    mag = np.broadcast_to(rows.astype(np.float32)[:, :, None], (4, BLK, 128)).copy()
    return k_pair, perm.astype(ml_dtypes.bfloat16), perm.T.copy().astype(ml_dtypes.bfloat16), mag


def device_index():
    return lax.axis_index("grp") * 64 + lax.axis_index("box")


def comm_kernel(
    owner_ref, coarse_ref, panels_ref, coarse_out, win_out, line, picked, crossed, win,
    send1, recv1, send2, recv2, send3, recv3,
):
    grp, box = lax.axis_index("grp"), lax.axis_index("box")
    row, col = box // 8, box % 8
    me = grp * 64 + box
    nxt, prv = lax.rem(me + 1, 512), lax.rem(me + 511, 512)
    cols = [row * 8 + lax.rem(col + r, 8) for r in range(1, 8)]
    rows = [lax.rem(row + r, 8) * 8 + col for r in range(1, 8)]
    beside = [(nxt // 64, nxt % 64), (prv // 64, prv % 64)]

    barrier = pltpu.get_barrier_semaphore()
    for other in cols + rows:
        pl.semaphore_signal(barrier, inc=1, device_id=(grp, other), device_id_type=MESH)
    for other in beside:
        pl.semaphore_signal(barrier, inc=1, device_id=other, device_id_type=MESH)
    line[col] = jnp.zeros((8, 128), F32)
    for r in range(6):
        width = min(128, NPTS - 128 * r)
        line[col, r : r + 1, 0:width] = coarse_ref[0:1, 128 * r : 128 * r + width]
    win[1] = panels_ref[...]
    pl.semaphore_wait(barrier, 16)

    first = []
    for r in range(1, 8):
        first.append(
            pltpu.make_async_remote_copy(
                src_ref=line.at[col], dst_ref=line.at[col], send_sem=send1.at[r - 1], recv_sem=recv1.at[r - 1],
                device_id=(grp, cols[r - 1]), device_id_type=MESH,
            )
        )
        first[-1].start()
    halo = []
    for r, other in enumerate(beside):
        halo.append(
            pltpu.make_async_remote_copy(
                src_ref=win.at[1], dst_ref=win.at[2 * r], send_sem=send3.at[r], recv_sem=recv3.at[r],
                device_id=other, device_id_type=MESH,
            )
        )
        halo[-1].start()
    for copy in first:
        copy.wait()
    for r in range(8):
        there = lax.rem(row + r, 8) * 8 + col
        want = jnp.bitwise_and(owner_ref[grp * 64 + there], 7)
        if r == 0:
            crossed[row] = line[want]
        else:
            picked[r] = line[want]
    second = []
    for r in range(1, 8):
        second.append(
            pltpu.make_async_remote_copy(
                src_ref=picked.at[r], dst_ref=crossed.at[row], send_sem=send2.at[r - 1], recv_sem=recv2.at[r - 1],
                device_id=(grp, rows[r - 1]), device_id_type=MESH,
            )
        )
        second[-1].start()
    for copy in halo:
        copy.wait()
    keep_low = jnp.where(me == 0, 0.0, 1.0)
    keep_high = jnp.where(me == 511, 0.0, 1.0)
    win_out[0] = win[0] * keep_low
    win_out[1] = win[1]
    win_out[2] = win[2] * keep_high
    for copy in second:
        copy.wait()
    slot = jnp.bitwise_and(owner_ref[me], 63)
    coarse_out[...] = crossed[jnp.right_shift(slot, 3)]


def exchange(owner_slot, coarse_row, panels):
    vmem = pl.BlockSpec(memory_space=pltpu.VMEM)
    return pl.pallas_call(
        comm_kernel,
        out_shape=(jax.ShapeDtypeStruct((8, 128), F32), jax.ShapeDtypeStruct((3, 4, 1024), F32)),
        in_specs=[pl.BlockSpec(memory_space=pltpu.SMEM), vmem, vmem],
        out_specs=(vmem, vmem),
        scratch_shapes=[
            pltpu.VMEM((8, 8, 128), F32),
            pltpu.VMEM((8, 8, 128), F32),
            pltpu.VMEM((8, 8, 128), F32),
            pltpu.VMEM((3, 4, 1024), F32),
            pltpu.SemaphoreType.DMA((7,)),
            pltpu.SemaphoreType.DMA((7,)),
            pltpu.SemaphoreType.DMA((7,)),
            pltpu.SemaphoreType.DMA((7,)),
            pltpu.SemaphoreType.DMA((2,)),
            pltpu.SemaphoreType.DMA((2,)),
        ],
        compiler_params=pltpu.CompilerParams(collective_id=0, has_side_effects=True),
        name="exchange",
    )(owner_slot, coarse_row, panels)


def pieces3(value):
    hi = value.astype(BF16).astype(F32)
    rest = value - hi
    mid = rest.astype(BF16).astype(F32)
    return hi, mid, (rest - mid).astype(BF16).astype(F32)


def mm(a, b):
    return jnp.dot(a, b, preferred_element_type=F32)


def compute_kernel(
    device_ref, part_s, pan_s, count_s, coarse_ref, m_ref, pown_ref, lown_ref, leaf_counts_ref, parts_ref, win_ref,
    k_ref, perm_ref, permt_ref, mag_ref, out_ref,
    m_full, m_pair, turn, pown, lown, hot, xrel, xf, xk, pf, pk, zb, acc, uexp,
):
    lane = lax.broadcasted_iota(jnp.int32, (1, 128), 1)
    device = device_ref[0]

    counts = leaf_counts_ref[...].astype(F32)
    g_row = lax.broadcasted_iota(jnp.int32, (64, 64), 0)
    g_col = lax.broadcasted_iota(jnp.int32, (64, 64), 1)
    upto = jnp.sum(jnp.where(g_col <= g_row, counts, 0.0), 1, keepdims=True)
    before = jnp.sum(jnp.where(g_col < g_row, counts, 0.0), 1, keepdims=True)
    leaf = lax.broadcasted_iota(jnp.int32, (64, 1), 0)
    local = []
    for a in range(3):
        c = jnp.bitwise_and(jnp.right_shift(leaf, a), 1) + 2 * jnp.bitwise_and(jnp.right_shift(leaf, 3 + a), 1)
        local.append((2 * c - 3).astype(F32))
    for n in range(16):
        index = (lax.broadcasted_iota(jnp.int32, (1, 128), 1) + 128 * n).astype(F32)
        inside = jnp.where((index >= before) & (index < upto), 1.0, 0.0)
        hot[n, 0:64] = inside.astype(BF16)
        hot[n, 64:128] = inside.astype(BF16)
        for a in range(3):
            centre = jnp.sum(inside * local[a], 0, keepdims=True)
            xrel[a : a + 1, 128 * n : 128 * n + 128] = parts_ref[a : a + 1, 128 * n : 128 * n + 128] + centre

    xf[...] = jnp.zeros_like(xf)
    pf[...] = jnp.zeros_like(pf)
    x = xrel[0:3, :]
    hi, mid, low = pieces3(x)
    for r, piece in enumerate((hi, mid, hi, low, hi, mid)):
        xf[3 * r : 3 * r + 3, :] = piece
    for r, piece in enumerate(pieces3(jnp.sum(x * x, 0, keepdims=True))):
        xf[18 + r : 19 + r, :] = piece
    xf[21:24, :] = jnp.ones((3, 2048), F32)
    for n in range(16):
        xk[n] = xf[:, 128 * n : 128 * n + 128].astype(BF16)
    axis = lax.broadcasted_iota(jnp.int32, (4, 1), 0)
    shift = jnp.zeros((4, 1), jnp.int32)
    for b in range(3):
        bit = jnp.bitwise_and(jnp.right_shift(device, 3 * b + axis), 1)
        shift = shift + jnp.left_shift(bit, b)
    centre = jnp.where(axis < 3, (8 * shift + 4).astype(F32), 0.0)
    for s in range(3):
        raw = win_ref[s] - centre
        at = slice(1024 * s, 1024 * s + 1024)
        z = raw[0:3]
        hi, mid, low = pieces3(z)
        for r, piece in enumerate((hi, hi, mid, hi, low, mid)):
            pf[3 * r : 3 * r + 3, at] = -2.0 * piece
        pf[18:21, at] = jnp.ones((3, 1024), F32)
        for r, piece in enumerate(pieces3(jnp.sum(z * z, 0, keepdims=True) + SOFTEN_SQ)):
            pf[21 + r : 22 + r, at] = piece
        pf[24:28, at] = raw

    def panel_tile(t, carry):
        block = pf[:, pl.ds(pl.multiple_of(t * 128, 128), 128)]
        turned = block.T
        pk[t] = turned[:, 0:32].astype(BF16)
        for a in range(4):
            zb[t, a] = jnp.broadcast_to(turned[:, 24 + a : 25 + a], (128, 128))
        return carry

    lax.fori_loop(0, 24, panel_tile, 0)

    acc[...] = jnp.zeros_like(acc)

    def near_slot(t, carry):
        to, tile = part_s[t], pan_s[t]
        r2 = mm(pk[tile], xk[to])
        sums = [jnp.zeros((8, 128), F32)] * 5
        for v in range(16):
            rows = slice(8 * v, 8 * v + 8)
            inv = lax.rsqrt(r2[rows])
            w = zb[tile, 3, rows] * inv
            w3 = w * (inv * inv)
            sums[0] = sums[0] + w
            sums[1] = sums[1] + w3
            for a in range(3):
                sums[2 + a] = sums[2 + a] + w3 * zb[tile, a, rows]
        for q in range(5):
            acc[to, q] += sums[q]
        return carry

    lax.fori_loop(0, count_s[0], near_slot, 0)

    m_full[NPTS:WID, :] = jnp.zeros((WID - NPTS, WID), F32)
    m_full[:, 640:WID] = jnp.zeros((WID, 128), F32)

    def m_copy(r, carry):
        rows = pl.ds(pl.multiple_of(r * 56, 8), 56)
        m_full[rows, 0:NPTS] = m_ref[rows, :]
        return carry

    lax.fori_loop(0, 13, m_copy, 0)

    def m_split(r, carry):
        rows = pl.ds(pl.multiple_of(r * 64, 64), 64)
        value = m_full[rows, :]
        hi = value.astype(BF16)
        m_pair[rows, 0:WID] = hi
        m_pair[rows, WID : 2 * WID] = (value - hi.astype(F32)).astype(BF16)
        return carry

    lax.fori_loop(0, 12, m_split, 0)

    turn[:, 640:WID] = jnp.zeros((128, 128), F32)
    for k in range(8):
        value = jnp.broadcast_to(pown_ref[k : k + 1, :], (8, NPTS))
        turn[8 * k : 8 * k + 8, 0:NPTS] = value
        turn[64 + 8 * k : 72 + 8 * k, 0:NPTS] = value
    pown[...] = turn[...].T
    turn[0:64, 0:NPTS] = lown_ref[...]
    turn[64:128, 0:NPTS] = lown_ref[...]
    lown[...] = turn[...].T

    low_half = lane < 64
    column = jnp.bitwise_and(lane, 63)

    def swapped(value, octant):
        blocks = [value[BLK * s : BLK * s + BLK] for s in range(8)]
        for b in range(3):
            mask = jnp.bitwise_and(jnp.right_shift(octant, b), 1) == 1
            blocks = [jnp.where(mask, blocks[s ^ (1 << b)], blocks[s]) for s in range(8)]
        return jnp.concatenate(blocks, 0)

    def pieces(value):
        hi = value.astype(BF16).astype(F32)
        return jnp.where(low_half, hi, value - hi).astype(BF16)

    def both(pair_ref, x2):
        product = mm(pair_ref[:, 0:WID], x2) + mm(pair_ref[:, WID : 2 * WID], x2)
        return product + pltpu.roll(product, 64, 1)

    def level(x2, octant, own):
        placed = swapped(x2, octant).astype(BF16)
        checks = swapped(both(k_ref, placed), octant)
        back = mm(permt_ref[...], pieces(checks)).astype(BF16)
        return both(m_pair, back) + own

    rows_hi, rows_lo = [], []
    row = lax.broadcasted_iota(jnp.int32, (128, 1), 0)
    spread = []
    for r in range(6):
        value = coarse_ref[r : r + 1, :]
        hi = value.astype(BF16).astype(F32)
        spread.append(jnp.where(row < 64, hi, value - hi))
    spread = jnp.concatenate(spread, 1).astype(BF16)
    start = lax.dot_general(perm_ref[...], spread, (((1,), (1,)), ((), ())), preferred_element_type=F32)
    parents = level(start, jnp.right_shift(column, 3), pown[...])
    placed = mm(perm_ref[...], pieces(parents))
    leaves = level(placed, jnp.bitwise_and(column, 7), lown[...])
    dens = mm(perm_ref[...], pieces(leaves)).astype(BF16)

    def far_tile(n, carry):
        uexp[...] = mm(dens, hot[n])
        at = pl.ds(pl.multiple_of(n * 128, 128), 128)
        y = [jnp.broadcast_to(parts_ref[a : a + 1, at], (8, 128)) for a in range(3)]
        y2 = y[0] * y[0] + y[1] * y[1] + y[2] * y[2]
        pot = jnp.zeros((8, 128), F32)
        total = [jnp.zeros((8, 128), F32)] * 4
        for v in range(BLK // 8):
            rows = slice(8 * v, 8 * v + 8)
            mags = [mag_ref[a, rows] for a in range(3)]
            part = [y2 + mag_ref[3, rows]]
            for a in range(3):
                step = y[a] * mags[a]
                part = [q + step for q in part] + [q - step for q in part]
            w3 = []
            for s in range(8):
                inv = lax.rsqrt(part[s])
                w = uexp[BLK * s + 8 * v : BLK * s + 8 * v + 8] * inv
                pot = pot + w
                w3.append(w * (inv * inv))
            x0 = [w3[s] + w3[s + 1] for s in (0, 2, 4, 6)]
            x1 = [w3[s + 1] - w3[s] for s in (0, 2, 4, 6)]
            y0 = [x0[s] + x0[s + 1] for s in (0, 2)]
            y1 = [x0[s + 1] - x0[s] for s in (0, 2)]
            total[0] = total[0] + (y0[0] + y0[1])
            total[1] = total[1] + ((x1[0] + x1[1]) + (x1[2] + x1[3])) * mags[0]
            total[2] = total[2] + (y1[0] + y1[1]) * mags[1]
            total[3] = total[3] + (y0[1] - y0[0]) * mags[2]
        near = [acc[n, q] for q in range(5)]
        scale = 1.0 / FOUR_PI
        out_ref[0:1, at] = scale * jnp.sum(pot + near[0], 0, keepdims=True)
        for a in range(3):
            whole = (y[a] * total[0] - 0.5 * total[1 + a]) + (xrel[a : a + 1, at] * near[1] - near[2 + a])
            out_ref[1 + a : 2 + a, at] = -scale * jnp.sum(whole, 0, keepdims=True)
        return carry

    lax.fori_loop(0, 16, far_tile, 0)


def evaluate(device, near_part, near_pan, near_count, coarse, m, pown, lown, leaf_counts, particles, window):
    vmem = pl.BlockSpec(memory_space=pltpu.VMEM)
    smem = pl.BlockSpec(memory_space=pltpu.SMEM)
    constants = [jnp.asarray(value) for value in tables()]
    return pl.pallas_call(
        compute_kernel,
        out_shape=jax.ShapeDtypeStruct((4, 2048), F32),
        in_specs=[smem] * 4 + [vmem] * 11,
        out_specs=vmem,
        scratch_shapes=[
            pltpu.VMEM((WID, WID), F32),
            pltpu.VMEM((WID, 2 * WID), BF16),
            pltpu.VMEM((128, WID), F32),
            pltpu.VMEM((WID, 128), F32),
            pltpu.VMEM((WID, 128), F32),
            pltpu.VMEM((16, 128, 128), BF16),
            pltpu.VMEM((8, 2048), F32),
            pltpu.VMEM((32, 2048), F32),
            pltpu.VMEM((16, 32, 128), BF16),
            pltpu.VMEM((128, 3072), F32),
            pltpu.VMEM((24, 128, 32), BF16),
            pltpu.VMEM((24, 4, 128, 128), F32),
            pltpu.VMEM((16, 5, 8, 128), F32),
            pltpu.VMEM((WID, 128), F32),
        ],
        compiler_params=pltpu.CompilerParams(vmem_limit_bytes=48 * 1024 * 1024),
        name="evaluate",
    )(device, near_part, near_pan, near_count, coarse, m, pown, lown, leaf_counts, particles, window, *constants)


def per_device(
    coarse_dens, owner_slot, check_to_equiv, parent_own, leaf_own, leaf_counts, particles, panels, near_part,
    near_pan, near_count,
):
    coarse, window = exchange(owner_slot, coarse_dens.T, panels)
    device = device_index().reshape(1)
    return evaluate(
        device, near_part, near_pan, near_count, coarse, check_to_equiv, parent_own.T, leaf_own.T, leaf_counts,
        particles, window,
    )


def solution(mesh):
    both = ("grp", "box")
    placed = (
        P(None, both), P(), P(), P(None, both), P(None, both), P(both, None), P(None, both), P(None, both), P(both),
        P(both), P(both),
    )
    return jax.shard_map(per_device, mesh=mesh, in_specs=placed, out_specs=P(None, both), check_vma=False)
```

```python
import functools
import math

import jax
import jax.numpy as jnp
import ml_dtypes
import numpy as np
from jax import lax
from jax.experimental import pallas as pl
from jax.experimental.pallas import tpu as pltpu
from jax.sharding import PartitionSpec as P

ORDER = 12
EQUIV_RADIUS = 2.95
CHECK_RADIUS = 1.05
SOFTEN_SQ = 0.0625
FOUR_PI = 4.0 * math.pi
MESH = pl.DeviceIdType.MESH

NPTS = 728
MAGS = 91
BLK = 96
WID = 8 * BLK
F32, BF16 = jnp.float32, jnp.bfloat16


def surface_points(edge_points):
    spacing = np.linspace(-1.0, 1.0, edge_points)
    lattice = np.stack(np.meshgrid(spacing, spacing, spacing, indexing="ij"), 0).reshape(3, -1)
    on_surface = np.max(np.abs(lattice), axis=0) > 0.999
    return lattice[:, on_surface].astype(np.float32)


def split2(value):
    hi = value.astype(ml_dtypes.bfloat16)
    lo = (value - hi.astype(np.float32)).astype(ml_dtypes.bfloat16)
    return hi, lo


@functools.lru_cache(maxsize=None)
def tables():
    points = surface_points(ORDER).astype(np.float64)
    grid = np.rint((points + 1.0) * (ORDER - 1) / 2.0).astype(int)
    index = {tuple(g): i for i, g in enumerate(grid.T)}
    half = ORDER // 2
    mags = [g for g in grid.T if min(g) >= half]
    order = np.full(WID, -1)
    for s in range(8):
        for m, g in enumerate(mags):
            key = tuple(g[a] if s >> a & 1 else ORDER - 1 - g[a] for a in range(3))
            order[BLK * s + m] = index[key]
    live = order >= 0
    placed = points[:, np.where(live, order, 0)]
    targets = -0.5 + 0.5 * CHECK_RADIUS * placed
    separation = targets[:, :, None] - EQUIV_RADIUS * placed[:, None, :]
    k0 = 1.0 / (FOUR_PI * np.sqrt(np.sum(separation * separation, 0)))
    k0 = np.where(live[:, None] & live[None, :], k0, 0.0).astype(np.float32)
    k_pair = np.concatenate(split2(k0), 1)
    perm = np.zeros((WID, WID), np.float32)
    perm[np.nonzero(live)[0], order[live]] = 1.0
    size = np.ones((3, BLK))
    size[:, :MAGS] = np.array([[points[a, index[tuple(g)]] for g in mags] for a in range(3)])
    rows = np.concatenate([2.0 * EQUIV_RADIUS * size, EQUIV_RADIUS**2 * np.sum(size * size, 0)[None]], 0)
    mag = np.broadcast_to(rows.astype(np.float32)[:, :, None], (4, BLK, 128)).copy()
    return k_pair, perm.astype(ml_dtypes.bfloat16), perm.T.copy().astype(ml_dtypes.bfloat16), mag


def pieces3(value):
    hi = value.astype(BF16).astype(F32)
    rest = value - hi
    mid = rest.astype(BF16).astype(F32)
    return hi, mid, (rest - mid).astype(BF16).astype(F32)


def mm(a, b):
    return jnp.dot(a, b, preferred_element_type=F32)


UNROLL = 4


def kernel(
    remote, *refs,
):
    if not remote:
        device_ref, coarse_in, win_in, *refs = refs
    (
        owner_ref, part_s, pan_s, count_s, tile_ref, counts_ref, coarse_hbm, panels_hbm, parts_hbm, pown_hbm, lown_hbm,
        m_hbm, k_hbm, perm_hbm, permt_hbm, mag_hbm, out_ref,
        coarse_ref, panels_ref, parts_ref, pown_ref, lown_ref, m_ref, k_ref, perm_ref, permt_ref, mag_ref, load_sem,
        line, picked, crossed, win, send1, recv1, send2, recv2, send3, recv3,
        m_pair, turn, pown, lown, hot, xrel, xf, xk, pf, pk, zb, slots, acc, uexp,
    ) = refs
    moves = {
        "coarse": (coarse_hbm, coarse_ref), "panels": (panels_hbm, panels_ref), "parts": (parts_hbm, parts_ref),
        "pown": (pown_hbm, pown_ref), "lown": (lown_hbm, lown_ref), "m": (m_hbm, m_ref.at[0:NPTS]),
        "k": (k_hbm, k_ref), "perm": (perm_hbm, perm_ref), "permt": (permt_hbm, permt_ref), "mag": (mag_hbm, mag_ref),
    }
    loads = {
        name: pltpu.make_async_copy(src, dst, load_sem.at[i]) for i, (name, (src, dst)) in enumerate(moves.items())
    }
    if remote:
        grp, box = lax.axis_index("grp"), lax.axis_index("box")
        row, col = box // 8, box % 8
        me = grp * 64 + box
        nxt, prv = lax.rem(me + 1, 512), lax.rem(me + 511, 512)
        cols = [row * 8 + lax.rem(col + r, 8) for r in range(1, 8)]
        rows = [lax.rem(row + r, 8) * 8 + col for r in range(1, 8)]
        beside = [(nxt // 64, nxt % 64), (prv // 64, prv % 64)]
        barrier = pltpu.get_barrier_semaphore()
        for other in cols + rows:
            pl.semaphore_signal(barrier, inc=1, device_id=(grp, other), device_id_type=MESH)
        for other in beside:
            pl.semaphore_signal(barrier, inc=1, device_id=other, device_id_type=MESH)
        device = me
    else:
        device = device_ref[0]
    for load in loads.values():
        load.start()

    first, halo, second = [], [], []
    loads["coarse"].wait()
    loads["panels"].wait()
    if remote:
        line[col] = jnp.zeros((8, 128), F32)
        for r in range(6):
            width = min(128, NPTS - 128 * r)
            line[col, r : r + 1, 0:width] = coarse_ref[0:1, 128 * r : 128 * r + width]
        win[1] = panels_ref[...]
        pl.semaphore_wait(barrier, 16)
        for r in range(1, 8):
            first.append(
                pltpu.make_async_remote_copy(
                    src_ref=line.at[col], dst_ref=line.at[col], send_sem=send1.at[r - 1], recv_sem=recv1.at[r - 1],
                    device_id=(grp, cols[r - 1]), device_id_type=MESH,
                )
            )
            first[-1].start()
        for r, other in enumerate(beside):
            halo.append(
                pltpu.make_async_remote_copy(
                    src_ref=win.at[1], dst_ref=win.at[2 * r], send_sem=send3.at[r], recv_sem=recv3.at[r],
                    device_id=other, device_id_type=MESH,
                )
            )
            halo[-1].start()
    else:
        for s in range(3):
            win[s] = win_in[s]

    lane = lax.broadcasted_iota(jnp.int32, (1, 128), 1)

    counts = counts_ref[...].astype(F32)
    g_row = lax.broadcasted_iota(jnp.int32, (64, 64), 0)
    g_col = lax.broadcasted_iota(jnp.int32, (64, 64), 1)
    upto = jnp.sum(jnp.where(g_col <= g_row, counts, 0.0), 1, keepdims=True)
    before = jnp.sum(jnp.where(g_col < g_row, counts, 0.0), 1, keepdims=True)
    leaf = lax.broadcasted_iota(jnp.int32, (64, 1), 0)
    local = []
    for a in range(3):
        c = jnp.bitwise_and(jnp.right_shift(leaf, a), 1) + 2 * jnp.bitwise_and(jnp.right_shift(leaf, 3 + a), 1)
        local.append((2 * c - 3).astype(F32))
    loads["parts"].wait()
    for n in range(16):
        index = (lax.broadcasted_iota(jnp.int32, (1, 128), 1) + 128 * n).astype(F32)
        inside = jnp.where((index >= before) & (index < upto), 1.0, 0.0)
        hot[n, 0:64] = inside.astype(BF16)
        hot[n, 64:128] = inside.astype(BF16)
        for a in range(3):
            centre = jnp.sum(inside * local[a], 0, keepdims=True)
            xrel[a : a + 1, 128 * n : 128 * n + 128] = parts_ref[a : a + 1, 128 * n : 128 * n + 128] + centre

    xf[...] = jnp.zeros_like(xf)
    x = xrel[0:3, :]
    hi, mid, low = pieces3(x)
    for r, piece in enumerate((hi, mid, hi, low, hi, mid)):
        xf[3 * r : 3 * r + 3, :] = piece
    for r, piece in enumerate(pieces3(jnp.sum(x * x, 0, keepdims=True))):
        xf[18 + r : 19 + r, :] = piece
    xf[21:24, :] = jnp.ones((3, 2048), F32)
    for n in range(16):
        xk[n] = xf[:, 128 * n : 128 * n + 128].astype(BF16)
    axis = lax.broadcasted_iota(jnp.int32, (4, 1), 0)
    shift = jnp.zeros((4, 1), jnp.int32)
    for b in range(3):
        bit = jnp.bitwise_and(jnp.right_shift(device, 3 * b + axis), 1)
        shift = shift + jnp.left_shift(bit, b)
    centre = jnp.where(axis < 3, (8 * shift + 4).astype(F32), 0.0)
    pf[28:128, :] = jnp.zeros((100, 1024), F32)

    def panel_part(s, keep):
        raw = win[s] * keep - centre
        z = raw[0:3]
        hi, mid, low = pieces3(z)
        for r, piece in enumerate((hi, hi, mid, hi, low, mid)):
            pf[3 * r : 3 * r + 3, :] = -2.0 * piece
        pf[18:21, :] = jnp.ones((3, 1024), F32)
        for r, piece in enumerate(pieces3(jnp.sum(z * z, 0, keepdims=True) + SOFTEN_SQ)):
            pf[21 + r : 22 + r, :] = piece
        pf[24:28, :] = raw

        for t in range(8):
            turned = pf[:, 128 * t : 128 * t + 128].T
            pk[8 * s + t] = turned[:, 0:32].astype(BF16)
            for a in range(4):
                zb[8 * s + t, a] = jnp.broadcast_to(turned[:, 24 + a : 25 + a], (128, 128))

    panel_part(1, 1.0)

    turn[:, 640:WID] = jnp.zeros((128, 128), F32)
    loads["pown"].wait()
    for k in range(8):
        value = jnp.broadcast_to(pown_ref[k : k + 1, :], (8, NPTS))
        turn[8 * k : 8 * k + 8, 0:NPTS] = value
        turn[64 + 8 * k : 72 + 8 * k, 0:NPTS] = value
    pown[...] = turn[...].T
    loads["lown"].wait()
    turn[0:64, 0:NPTS] = lown_ref[...]
    turn[64:128, 0:NPTS] = lown_ref[...]
    lown[...] = turn[...].T

    if remote:
        for copy in first:
            copy.wait()
        for r in range(8):
            there = lax.rem(row + r, 8) * 8 + col
            want = jnp.bitwise_and(owner_ref[grp * 64 + there], 7)
            if r == 0:
                crossed[row] = line[want]
            else:
                picked[r] = line[want]
        for r in range(1, 8):
            second.append(
                pltpu.make_async_remote_copy(
                    src_ref=picked.at[r], dst_ref=crossed.at[row], send_sem=send2.at[r - 1],
                    recv_sem=recv2.at[r - 1], device_id=(grp, rows[r - 1]), device_id_type=MESH,
                )
            )
            second[-1].start()

    m_pair[:, 640:WID] = jnp.zeros((WID, 128), BF16)
    m_pair[:, WID + 640 : 2 * WID] = jnp.zeros((WID, 128), BF16)
    m_ref[NPTS:WID] = jnp.zeros((WID - NPTS, NPTS), F32)
    loads["m"].wait()

    def m_split(r, carry):
        at = pl.ds(pl.multiple_of(r * 64, 64), 64)
        value = m_ref[at, :]
        hi = value.astype(BF16)
        m_pair[at, 0:NPTS] = hi
        m_pair[at, WID : WID + NPTS] = (value - hi.astype(F32)).astype(BF16)
        return carry

    lax.fori_loop(0, 12, m_split, 0)

    for copy in halo:
        copy.wait()
    panel_part(0, jnp.where(device == 0, 0.0, 1.0))
    panel_part(2, jnp.where(device == 511, 0.0, 1.0))

    def near_slots(i, carry):
        where = [i * UNROLL + u for u in range(UNROLL)]
        tiles = [pan_s[t] for t in where]
        squares = [mm(pk[tiles[u]], xk[part_s[where[u]]]) for u in range(UNROLL)]
        for u in range(UNROLL):
            sums = [jnp.zeros((8, 128), F32)] * 5
            z = [zb[tiles[u], a] for a in range(4)]
            for v in range(16):
                at = slice(8 * v, 8 * v + 8)
                inv = lax.rsqrt(squares[u][at])
                w = z[3][at] * inv
                w3 = w * (inv * inv)
                sums[0] = sums[0] + w
                sums[1] = sums[1] + w3
                for a in range(3):
                    sums[2 + a] = sums[2 + a] + w3 * z[a][at]
            at = pl.ds(pl.multiple_of(where[u] * 8, 8), 8)
            for q in range(5):
                slots[at, 128 * q : 128 * q + 128] = sums[q]
        return carry

    lax.fori_loop(0, 64 // UNROLL, near_slots, 0)
    slot = lax.broadcasted_iota(jnp.int32, (1, 64), 1)
    live = jnp.where(slot < count_s[0], tile_ref[...], 31).astype(F32)
    e_row = lax.broadcasted_iota(jnp.int32, (64, 512), 0)
    e_col = lax.broadcasted_iota(jnp.int32, (64, 512), 1)
    spread8 = jnp.where(jnp.right_shift(e_col, 3) == e_row, 1.0, 0.0).astype(BF16)
    target = mm(jnp.broadcast_to(live, (16, 64)).astype(BF16), spread8)
    n_row = lax.broadcasted_iota(jnp.int32, (16, 512), 0).astype(F32)
    choose = jnp.where(target == n_row, 1.0, 0.0).astype(BF16)
    hi, mid, low = pieces3(slots[...])
    acc[...] = mm(choose, hi.astype(BF16)) + (mm(choose, mid.astype(BF16)) + mm(choose, low.astype(BF16)))

    low_half = lane < 64
    column = jnp.bitwise_and(lane, 63)

    def swapped(value, octant):
        blocks = [value[BLK * s : BLK * s + BLK] for s in range(8)]
        for b in range(3):
            mask = jnp.bitwise_and(jnp.right_shift(octant, b), 1) == 1
            blocks = [jnp.where(mask, blocks[s ^ (1 << b)], blocks[s]) for s in range(8)]
        return jnp.concatenate(blocks, 0)

    def pieces(value):
        hi = value.astype(BF16).astype(F32)
        return jnp.where(low_half, hi, value - hi).astype(BF16)

    def both(pair_ref, x2):
        product = mm(pair_ref[:, 0:WID], x2) + mm(pair_ref[:, WID : 2 * WID], x2)
        return product + pltpu.roll(product, 64, 1)

    def level(x2, octant, own):
        placed = swapped(x2, octant).astype(BF16)
        checks = swapped(both(k_ref, placed), octant)
        back = mm(permt_ref[...], pieces(checks)).astype(BF16)
        return both(m_pair, back) + own

    loads["perm"].wait()
    loads["k"].wait()
    loads["permt"].wait()
    loads["mag"].wait()
    if remote:
        for copy in second:
            copy.wait()
        slot = jnp.bitwise_and(owner_ref[me], 63)
        coarse = crossed[jnp.right_shift(slot, 3)]
    else:
        coarse = coarse_in[...]
    half = lax.broadcasted_iota(jnp.int32, (128, 1), 0) < 64
    spread = []
    for r in range(6):
        value = coarse[r : r + 1, :]
        hi = value.astype(BF16).astype(F32)
        spread.append(jnp.where(half, hi, value - hi))
    spread = jnp.concatenate(spread, 1).astype(BF16)
    start = lax.dot_general(perm_ref[...], spread, (((1,), (1,)), ((), ())), preferred_element_type=F32)
    parents = level(start, jnp.right_shift(column, 3), pown[...])
    placed = mm(perm_ref[...], pieces(parents))
    leaves = level(placed, jnp.bitwise_and(column, 7), lown[...])
    dens = mm(perm_ref[...], pieces(leaves)).astype(BF16)

    def far_tile(n, carry):
        uexp[...] = mm(dens, hot[n])
        at = pl.ds(pl.multiple_of(n * 128, 128), 128)
        y = [jnp.broadcast_to(parts_ref[a : a + 1, at], (8, 128)) for a in range(3)]
        y2 = y[0] * y[0] + y[1] * y[1] + y[2] * y[2]
        pot = jnp.zeros((8, 128), F32)
        total = [jnp.zeros((8, 128), F32)] * 4
        for v in range(BLK // 8):
            band = slice(8 * v, 8 * v + 8)
            mags = [mag_ref[a, band] for a in range(3)]
            part = [y2 + mag_ref[3, band]]
            for a in range(3):
                step = y[a] * mags[a]
                part = [q + step for q in part] + [q - step for q in part]
            w3 = []
            for s in range(8):
                inv = lax.rsqrt(part[s])
                w = uexp[BLK * s + 8 * v : BLK * s + 8 * v + 8] * inv
                pot = pot + w
                w3.append(w * (inv * inv))
            x0 = [w3[s] + w3[s + 1] for s in (0, 2, 4, 6)]
            x1 = [w3[s + 1] - w3[s] for s in (0, 2, 4, 6)]
            y0 = [x0[s] + x0[s + 1] for s in (0, 2)]
            y1 = [x0[s + 1] - x0[s] for s in (0, 2)]
            total[0] = total[0] + (y0[0] + y0[1])
            total[1] = total[1] + ((x1[0] + x1[1]) + (x1[2] + x1[3])) * mags[0]
            total[2] = total[2] + (y1[0] + y1[1]) * mags[1]
            total[3] = total[3] + (y0[1] - y0[0]) * mags[2]
        mine = lax.broadcasted_iota(jnp.int32, (16, 128), 0) == n
        near = [
            jnp.sum(jnp.where(mine, acc[:, 128 * q : 128 * q + 128], 0.0), 0, keepdims=True) for q in range(5)
        ]
        scale = 1.0 / FOUR_PI
        out_ref[0:1, at] = scale * (jnp.sum(pot, 0, keepdims=True) + near[0])
        for a in range(3):
            whole = jnp.sum(y[a] * total[0] - 0.5 * total[1 + a], 0, keepdims=True)
            out_ref[1 + a : 2 + a, at] = -scale * (whole + (xrel[a : a + 1, at] * near[1] - near[2 + a]))
        return carry

    lax.fori_loop(0, 16, far_tile, 0)


def run(remote, *args):
    vmem = pl.BlockSpec(memory_space=pltpu.VMEM)
    smem = pl.BlockSpec(memory_space=pltpu.SMEM)
    anys = pl.BlockSpec(memory_space=pl.ANY)
    constants = [jnp.asarray(value) for value in tables()]
    dma = pltpu.SemaphoreType.DMA
    return pl.pallas_call(
        functools.partial(kernel, remote),
        out_shape=jax.ShapeDtypeStruct((4, 2048), F32),
        in_specs=([] if remote else [smem, vmem, vmem]) + [smem] * 4 + [vmem] * 2 + [anys] * 10,
        out_specs=vmem,
        scratch_shapes=[
            pltpu.VMEM((1, NPTS), F32),
            pltpu.VMEM((4, 1024), F32),
            pltpu.VMEM((3, 2048), F32),
            pltpu.VMEM((8, NPTS), F32),
            pltpu.VMEM((64, NPTS), F32),
            pltpu.VMEM((WID, NPTS), F32),
            pltpu.VMEM((WID, 2 * WID), BF16),
            pltpu.VMEM((WID, WID), BF16),
            pltpu.VMEM((WID, WID), BF16),
            pltpu.VMEM((4, BLK, 128), F32),
            dma((10,)),
            pltpu.VMEM((8, 8, 128), F32),
            pltpu.VMEM((8, 8, 128), F32),
            pltpu.VMEM((8, 8, 128), F32),
            pltpu.VMEM((3, 4, 1024), F32),
            dma((7,)),
            dma((7,)),
            dma((7,)),
            dma((7,)),
            dma((2,)),
            dma((2,)),
            pltpu.VMEM((WID, 2 * WID), BF16),
            pltpu.VMEM((128, WID), F32),
            pltpu.VMEM((WID, 128), F32),
            pltpu.VMEM((WID, 128), F32),
            pltpu.VMEM((16, 128, 128), BF16),
            pltpu.VMEM((8, 2048), F32),
            pltpu.VMEM((32, 2048), F32),
            pltpu.VMEM((16, 32, 128), BF16),
            pltpu.VMEM((128, 1024), F32),
            pltpu.VMEM((24, 128, 32), BF16),
            pltpu.VMEM((24, 4, 128, 128), F32),
            pltpu.VMEM((512, 640), F32),
            pltpu.VMEM((16, 640), F32),
            pltpu.VMEM((WID, 128), F32),
        ],
        compiler_params=pltpu.CompilerParams(
            vmem_limit_bytes=56 * 1024 * 1024, **(dict(collective_id=0, has_side_effects=True) if remote else {})
        ),
        name="downward",
    )(*args, *constants)


def per_device(
    coarse_dens, owner_slot, check_to_equiv, parent_own, leaf_own, leaf_counts, particles, panels, near_part,
    near_pan, near_count,
):
    return run(
        True, owner_slot, near_part, near_pan, near_count, near_part.reshape(1, 64), leaf_counts, coarse_dens.T, panels,
        particles, parent_own.T, leaf_own.T, check_to_equiv,
    )


def solution(mesh):
    both = ("grp", "box")
    placed = (
        P(None, both), P(), P(), P(None, both), P(None, both), P(both, None), P(None, both), P(None, both), P(both),
        P(both), P(both),
    )
    return jax.shard_map(per_device, mesh=mesh, in_specs=placed, out_specs=P(None, both), check_vma=False)
```

```python
import functools
import math

import jax
import jax.numpy as jnp
import ml_dtypes
import numpy as np
from jax import lax
from jax.experimental import pallas as pl
from jax.experimental.pallas import tpu as pltpu
from jax.sharding import PartitionSpec as P

ORDER = 12
EQUIV_RADIUS = 2.95
CHECK_RADIUS = 1.05
SOFTEN_SQ = 0.0625
FOUR_PI = 4.0 * math.pi
MESH = pl.DeviceIdType.MESH

NPTS = 728
MAGS = 91
BLK = 96
WID = 8 * BLK
F32, BF16 = jnp.float32, jnp.bfloat16


def surface_points(edge_points):
    spacing = np.linspace(-1.0, 1.0, edge_points)
    lattice = np.stack(np.meshgrid(spacing, spacing, spacing, indexing="ij"), 0).reshape(3, -1)
    on_surface = np.max(np.abs(lattice), axis=0) > 0.999
    return lattice[:, on_surface].astype(np.float32)


def split2(value):
    hi = value.astype(ml_dtypes.bfloat16)
    lo = (value - hi.astype(np.float32)).astype(ml_dtypes.bfloat16)
    return hi, lo


@functools.lru_cache(maxsize=None)
def tables():
    points = surface_points(ORDER).astype(np.float64)
    grid = np.rint((points + 1.0) * (ORDER - 1) / 2.0).astype(int)
    index = {tuple(g): i for i, g in enumerate(grid.T)}
    half = ORDER // 2
    mags = [g for g in grid.T if min(g) >= half]
    order = np.full(WID, -1)
    for s in range(8):
        for m, g in enumerate(mags):
            key = tuple(g[a] if s >> a & 1 else ORDER - 1 - g[a] for a in range(3))
            order[BLK * s + m] = index[key]
    live = order >= 0
    placed = points[:, np.where(live, order, 0)]
    targets = -0.5 + 0.5 * CHECK_RADIUS * placed
    separation = targets[:, :, None] - EQUIV_RADIUS * placed[:, None, :]
    k0 = 1.0 / (FOUR_PI * np.sqrt(np.sum(separation * separation, 0)))
    k0 = np.where(live[:, None] & live[None, :], k0, 0.0).astype(np.float32)
    k_pair = np.concatenate(split2(k0), 1)
    perm = np.zeros((WID, WID), np.float32)
    perm[np.nonzero(live)[0], order[live]] = 1.0
    size = np.ones((3, BLK))
    size[:, :MAGS] = np.array([[points[a, index[tuple(g)]] for g in mags] for a in range(3)])
    rows = np.concatenate([2.0 * EQUIV_RADIUS * size, EQUIV_RADIUS**2 * np.sum(size * size, 0)[None]], 0)
    mag = np.broadcast_to(rows.astype(np.float32)[:, :, None], (4, BLK, 128)).copy()
    return k_pair, perm.astype(ml_dtypes.bfloat16), perm.T.copy().astype(ml_dtypes.bfloat16), mag


def pieces3(value):
    hi = value.astype(BF16).astype(F32)
    rest = value - hi
    mid = rest.astype(BF16).astype(F32)
    return hi, mid, (rest - mid).astype(BF16).astype(F32)


def mm(a, b):
    return jnp.dot(a, b, preferred_element_type=F32)


UNROLL = 4


def kernel(
    remote, *refs,
):
    if not remote:
        device_ref, coarse_in, win_in, *refs = refs
    (
        owner_hbm, part_hbm, pan_hbm, count_hbm, tile_hbm, counts_hbm, coarse_hbm, panels_hbm, parts_hbm, pown_hbm, lown_hbm,
        m_hbm, k_hbm, perm_hbm, permt_hbm, mag_hbm, out_ref,
        owner_ref, part_s, pan_s, count_ref, tile_ref, counts_ref, coarse_ref, panels_ref, parts_ref, pown_ref, lown_ref, m_ref, k_ref, perm_ref, permt_ref, mag_ref, load_sem,
        line, picked, crossed, win, send1, recv1, send2, recv2, send3, recv3,
        m_half, m_pair, turn, pown, lown, hot, xrel, xf, xk, pf, pk, zb, slots, acc, uexp0, uexp1, sq0, sq1,
    ) = refs
    moves = {
        "coarse": (coarse_hbm, coarse_ref), "panels": (panels_hbm, panels_ref), "owner": (owner_hbm, owner_ref),
        "counts": (counts_hbm, counts_ref), "parts": (parts_hbm, parts_ref), "part": (part_hbm, part_s),
        "pan": (pan_hbm, pan_s), "count": (count_hbm, count_ref), "tile": (tile_hbm, tile_ref), "pown": (pown_hbm, pown_ref), "lown": (lown_hbm, lown_ref), "m": (m_hbm, m_ref.at[0:NPTS]),
        "permt": (permt_hbm, permt_ref), "perm": (perm_hbm, perm_ref), "k": (k_hbm, k_ref), "mag": (mag_hbm, mag_ref),
    }
    loads = {
        name: pltpu.make_async_copy(src, dst, load_sem.at[i]) for i, (name, (src, dst)) in enumerate(moves.items())
    }
    if remote:
        grp, box = lax.axis_index("grp"), lax.axis_index("box")
        row, col = box // 8, box % 8
        me = grp * 64 + box
        nxt, prv = lax.rem(me + 1, 512), lax.rem(me + 511, 512)
        cols = [row * 8 + lax.rem(col + r, 8) for r in range(1, 8)]
        rows = [lax.rem(row + r, 8) * 8 + col for r in range(1, 8)]
        beside = [(nxt // 64, nxt % 64), (prv // 64, prv % 64)]
        there = [me < 511, me > 0]
        greet = [jnp.logical_and(there[0], box != 63), there[1]]
        hear = [there[0], jnp.logical_and(there[1], box != 0)]
        answer = jnp.logical_and(there[1], box == 0)
        barrier = pltpu.get_barrier_semaphore()
        for other in rows + cols:
            pl.semaphore_signal(barrier, inc=1, device_id=(grp, other), device_id_type=MESH)
        for r in range(2):

            @pl.when(greet[r])
            def _(r=r):
                pl.semaphore_signal(barrier, inc=1, device_id=beside[r], device_id_type=MESH)

        device = me
    else:
        device = device_ref[0]
    for load in loads.values():
        load.start()
    if remote:
        first = [
            pltpu.make_async_remote_copy(
                src_ref=line.at[row], dst_ref=line.at[row], send_sem=send1.at[r], recv_sem=recv1.at[r],
                device_id=(grp, rows[r]), device_id_type=MESH,
            )
            for r in range(7)
        ]
        second = [
            pltpu.make_async_remote_copy(
                src_ref=picked.at[r], dst_ref=crossed.at[col], send_sem=send2.at[r], recv_sem=recv2.at[r],
                device_id=(grp, cols[r]), device_id_type=MESH,
            )
            for r in range(7)
        ]
        halo = [
            pltpu.make_async_remote_copy(
                src_ref=win.at[1], dst_ref=win.at[2 * r], send_sem=send3.at[r], recv_sem=recv3.at[r],
                device_id=beside[r], device_id_type=MESH,
            )
            for r in range(2)
        ]
    loads["coarse"].wait()
    loads["panels"].wait()
    loads["owner"].wait()
    if remote:
        line[row] = jnp.zeros((8, 128), F32)
        for r in range(6):
            width = min(128, NPTS - 128 * r)
            line[row, r : r + 1, 0:width] = coarse_ref[0:1, 128 * r : 128 * r + width]
        win[1] = panels_ref[...]
    else:
        for s in range(3):
            win[s] = win_in[s]

    lane = lax.broadcasted_iota(jnp.int32, (1, 128), 1)

    axis = lax.broadcasted_iota(jnp.int32, (4, 1), 0)
    shift = jnp.zeros((4, 1), jnp.int32)
    for b in range(3):
        bit = jnp.bitwise_and(jnp.right_shift(device, 3 * b + axis), 1)
        shift = shift + jnp.left_shift(bit, b)
    centre = jnp.where(axis < 3, (8 * shift + 4).astype(F32), 0.0)

    def panel_part(s):
        raw = win[s] - centre
        z = raw[0:3]
        hi, mid, low = pieces3(z)
        for r, piece in enumerate((hi, hi, mid, hi, low, mid)):
            pf[3 * r : 3 * r + 3, :] = -2.0 * piece
        pf[18:21, :] = jnp.ones((3, 1024), F32)
        for r, piece in enumerate(pieces3(jnp.sum(z * z, 0, keepdims=True) + SOFTEN_SQ)):
            pf[21 + r : 22 + r, :] = piece
        pf[24:28, :] = raw

        for t in range(8):
            turned = pf[:, 128 * t : 128 * t + 128].T
            operand = turned[:, 0:32].astype(BF16)
            pk[8 * s + t] = jnp.zeros((128, 128), BF16)
            pk[8 * s + t, :, 0:32] = operand
            pk[8 * s + t, :, 64:96] = operand
            for a in range(4):
                zb[8 * s + t, a] = jnp.broadcast_to(turned[:, 24 + a : 25 + a], (128, 128))

    def prepare():
        loads["counts"].wait()
        counts = counts_ref[...].astype(F32)
        g_row = lax.broadcasted_iota(jnp.int32, (64, 64), 0)
        g_col = lax.broadcasted_iota(jnp.int32, (64, 64), 1)
        upto = jnp.sum(jnp.where(g_col <= g_row, counts, 0.0), 1, keepdims=True)
        before = jnp.sum(jnp.where(g_col < g_row, counts, 0.0), 1, keepdims=True)
        leaf = lax.broadcasted_iota(jnp.int32, (64, 1), 0)
        local = []
        for a in range(3):
            c = jnp.bitwise_and(jnp.right_shift(leaf, a), 1) + 2 * jnp.bitwise_and(jnp.right_shift(leaf, 3 + a), 1)
            local.append((2 * c - 3).astype(F32))
        loads["parts"].wait()
        for n in range(16):
            index = (lax.broadcasted_iota(jnp.int32, (1, 128), 1) + 128 * n).astype(F32)
            inside = jnp.where((index >= before) & (index < upto), 1.0, 0.0)
            side = slice(128 * (n % 2), 128 * (n % 2) + 128)
            hot[n // 2, 0:64, side] = inside.astype(BF16)
            hot[n // 2, 64:128, side] = inside.astype(BF16)
            for a in range(3):
                centre = jnp.sum(inside * local[a], 0, keepdims=True)
                xrel[a : a + 1, 128 * n : 128 * n + 128] = parts_ref[a : a + 1, 128 * n : 128 * n + 128] + centre

        xf[...] = jnp.zeros_like(xf)
        x = xrel[0:3, :]
        hi, mid, low = pieces3(x)
        for r, piece in enumerate((hi, mid, hi, low, hi, mid)):
            xf[3 * r : 3 * r + 3, :] = piece
        for r, piece in enumerate(pieces3(jnp.sum(x * x, 0, keepdims=True))):
            xf[18 + r : 19 + r, :] = piece
        xf[21:24, :] = jnp.ones((3, 2048), F32)
        for n in range(16):
            xk[n] = xf[:, 128 * n : 128 * n + 128].astype(BF16)
        pf[28:128, :] = jnp.zeros((100, 1024), F32)
        panel_part(1)

        loads["perm"].wait()

        def placed_own():
            value = turn[...]
            hi = value.astype(BF16).astype(F32)
            both = jnp.where(lax.broadcasted_iota(jnp.int32, (128, 1), 0) < 64, hi, value - hi).astype(BF16)
            product = lax.dot_general(perm_ref[...], both, (((1,), (1,)), ((), ())), preferred_element_type=F32)
            return product + pltpu.roll(product, 64, 1)

        turn[:, 640:WID] = jnp.zeros((128, 128), F32)
        loads["pown"].wait()
        for k in range(8):
            value = jnp.broadcast_to(pown_ref[k : k + 1, :], (8, NPTS))
            turn[8 * k : 8 * k + 8, 0:NPTS] = value
            turn[64 + 8 * k : 72 + 8 * k, 0:NPTS] = value
        pown[...] = placed_own()
        loads["lown"].wait()
        turn[0:64, 0:NPTS] = lown_ref[...]
        turn[64:128, 0:NPTS] = lown_ref[...]
        lown[...] = placed_own()


    def prepare_m():
        m_ref[NPTS:WID] = jnp.zeros((WID - NPTS, NPTS), F32)
        loads["m"].wait()
        loads["permt"].wait()
        m_half[:, 640:WID] = jnp.zeros((WID, 128), BF16)
        m_half[:, WID + 640 : 2 * WID] = jnp.zeros((WID, 128), BF16)

        def m_split(r, carry):
            at = pl.ds(pl.multiple_of(r * 64, 64), 64)
            value = m_ref[at, :]
            hi = value.astype(BF16)
            m_half[at, 0:NPTS] = hi
            m_half[at, WID : WID + NPTS] = (value - hi.astype(F32)).astype(BF16)
            return carry

        lax.fori_loop(0, 12, m_split, 0)

        def m_columns(r, carry):
            at = pl.ds(pl.multiple_of(r * 256, 256), 256)
            for side in (slice(0, WID), slice(WID, 2 * WID)):
                m_half[at, side] = mm(m_half[at, side], permt_ref[...]).astype(BF16)
            return carry

        lax.fori_loop(0, 3, m_columns, 0)

        def m_rows(r, carry):
            at = pl.ds(pl.multiple_of(r * 256, 256), 256)
            m_pair[:, at] = mm(perm_ref[...], m_half[:, at]).astype(BF16)
            return carry

        lax.fori_loop(0, 6, m_rows, 0)


    if remote:
        early = box < 32

        @pl.when(early)
        def _():
            prepare()
            prepare_m()

        pl.semaphore_wait(barrier, 14 + hear[0].astype(jnp.int32) + hear[1].astype(jnp.int32))
        for copy in first:
            copy.start()
        for r in range(2):
            pl.when(hear[r])(halo[r].start)

        @pl.when(jnp.logical_not(early))
        def _():
            prepare()
            prepare_m()

        for copy in first:
            copy.wait()
        for r in range(8):
            whose = row * 8 + lax.rem(col + r, 8)
            want = jnp.bitwise_and(jnp.right_shift(owner_ref[grp * 64 + whose], 3), 7)
            if r == 0:
                crossed[col] = line[want]
            else:
                picked[r - 1] = line[want]
        for copy in second:
            copy.start()
        pl.when(there[1])(halo[0].wait_recv)
        pl.when(answer)(halo[1].start)
        pl.when(there[0])(halo[1].wait_recv)
        for r in range(2):
            pl.when(there[r])(halo[r].wait_send)

        @pl.when(jnp.logical_not(there[1]))
        def _():
            win[0] = jnp.zeros((4, 1024), F32)

        @pl.when(jnp.logical_not(there[0]))
        def _():
            win[2] = jnp.zeros((4, 1024), F32)

        panel_part(0)
        panel_part(2)
    else:
        prepare()
        prepare_m()
        panel_part(0)
        panel_part(2)

    loads["part"].wait()
    loads["pan"].wait()
    left = lax.broadcasted_iota(jnp.int32, (128, 128), 1) < 64
    blank = jnp.zeros((32, 128), BF16)

    def near_squares(i, into):
        for u in range(UNROLL // 2):
            t = i * UNROLL + 2 * u
            panel = jnp.where(left, pk[pan_s[t]], pk[pan_s[t + 1]])[:, 0:96]
            one, two = xk[part_s[t]], xk[part_s[t + 1]]
            part = jnp.concatenate(
                [jnp.concatenate([one, blank, blank], 0), jnp.concatenate([blank, blank, two], 0)], 1
            )
            into[u] = mm(panel, part)

    def near_sums(i, squares):
        for u in range(UNROLL):
            t = i * UNROLL + u
            tile = pan_s[t]
            side = slice(128 * (u % 2), 128 * (u % 2) + 128)
            sums = [jnp.zeros((8, 128), F32)] * 5
            for v in range(16):
                at = slice(8 * v, 8 * v + 8)
                inv = lax.rsqrt(squares[u // 2, at, side])
                w = zb[tile, 3, at] * inv
                w3 = w * (inv * inv)
                sums[0] = sums[0] + w
                sums[1] = sums[1] + w3
                for a in range(3):
                    sums[2 + a] = sums[2 + a] + w3 * zb[tile, a, at]
            at = pl.ds(pl.multiple_of(t * 8, 8), 8)
            for q in range(5):
                slots[at, 128 * q : 128 * q + 128] = sums[q]

    near_squares(0, sq0)
    steps = 64 // UNROLL

    def near_slots(i, carry):
        near_squares(2 * i + 1, sq1)
        near_sums(2 * i, sq0)
        near_squares(jnp.minimum(2 * i + 2, steps - 1), sq0)
        near_sums(2 * i + 1, sq1)
        return carry

    lax.fori_loop(0, steps // 2, near_slots, 0)
    loads["count"].wait()
    loads["tile"].wait()
    slot = lax.broadcasted_iota(jnp.int32, (1, 64), 1)
    live = jnp.where(slot < count_ref[0], tile_ref[...], 31).astype(F32)
    e_row = lax.broadcasted_iota(jnp.int32, (64, 512), 0)
    e_col = lax.broadcasted_iota(jnp.int32, (64, 512), 1)
    spread8 = jnp.where(jnp.right_shift(e_col, 3) == e_row, 1.0, 0.0).astype(BF16)
    target = mm(jnp.broadcast_to(live, (16, 64)).astype(BF16), spread8)
    n_row = lax.broadcasted_iota(jnp.int32, (16, 512), 0).astype(F32)
    choose = jnp.where(target == n_row, 1.0, 0.0).astype(BF16)
    hi, mid, low = pieces3(slots[...])
    acc[...] = mm(choose, hi.astype(BF16)) + (mm(choose, mid.astype(BF16)) + mm(choose, low.astype(BF16)))

    low_half = lane < 64
    column = jnp.bitwise_and(lane, 63)

    def swapped(value, octant):
        blocks = [value[BLK * s : BLK * s + BLK] for s in range(8)]
        for b in range(3):
            mask = jnp.bitwise_and(jnp.right_shift(octant, b), 1) == 1
            blocks = [jnp.where(mask, blocks[s ^ (1 << b)], blocks[s]) for s in range(8)]
        return jnp.concatenate(blocks, 0)

    def pieces(value):
        hi = value.astype(BF16).astype(F32)
        return jnp.where(low_half, hi, value - hi).astype(BF16)

    def both(pair_ref, x2):
        product = mm(pair_ref[...], jnp.concatenate([x2, x2], 0))
        return product + pltpu.roll(product, 64, 1)

    def level(x2, octant, own):
        checks = swapped(pieces(both(k_ref, swapped(x2, octant))), octant)
        return both(m_pair, checks) + own

    loads["k"].wait()
    loads["mag"].wait()
    if remote:
        for copy in second:
            copy.wait()
        slot = jnp.bitwise_and(owner_ref[me], 7)
        coarse = crossed[slot]
    else:
        coarse = coarse_in[...]
    half = lax.broadcasted_iota(jnp.int32, (128, 1), 0) < 64
    spread = []
    for r in range(6):
        value = coarse[r : r + 1, :]
        hi = value.astype(BF16).astype(F32)
        spread.append(jnp.where(half, hi, value - hi))
    spread = jnp.concatenate(spread, 1).astype(BF16)
    start = lax.dot_general(perm_ref[...], spread, (((1,), (1,)), ((), ())), preferred_element_type=F32)
    parents = level(start.astype(BF16), jnp.right_shift(column, 3), pown[...])
    leaves = level(pieces(parents), jnp.bitwise_and(column, 7), lown[...])
    dens = pieces(leaves)

    def far_tile(n, dense, side):
        at = pl.ds(pl.multiple_of(n * 128, 128), 128)
        y = [jnp.broadcast_to(parts_ref[a : a + 1, at], (8, 128)) for a in range(3)]
        y2 = y[0] * y[0] + y[1] * y[1] + y[2] * y[2]
        pot = jnp.zeros((8, 128), F32)
        total = [jnp.zeros((8, 128), F32)] * 4
        for v in range(BLK // 8):
            band = slice(8 * v, 8 * v + 8)
            mags = [mag_ref[a, band] for a in range(3)]
            part = [y2 + mag_ref[3, band]]
            for a in range(3):
                step = y[a] * mags[a]
                part = [q + step for q in part] + [q - step for q in part]
            w3 = []
            for s in range(8):
                inv = lax.rsqrt(part[s])
                w = dense[BLK * s + 8 * v : BLK * s + 8 * v + 8, side] * inv
                pot = pot + w
                w3.append(w * (inv * inv))
            x0 = [w3[s] + w3[s + 1] for s in (0, 2, 4, 6)]
            x1 = [w3[s + 1] - w3[s] for s in (0, 2, 4, 6)]
            y0 = [x0[s] + x0[s + 1] for s in (0, 2)]
            y1 = [x0[s + 1] - x0[s] for s in (0, 2)]
            total[0] = total[0] + (y0[0] + y0[1])
            total[1] = total[1] + ((x1[0] + x1[1]) + (x1[2] + x1[3])) * mags[0]
            total[2] = total[2] + (y1[0] + y1[1]) * mags[1]
            total[3] = total[3] + (y0[1] - y0[0]) * mags[2]
        mine = lax.broadcasted_iota(jnp.int32, (16, 128), 0) == n
        near = [
            jnp.sum(jnp.where(mine, acc[:, 128 * q : 128 * q + 128], 0.0), 0, keepdims=True) for q in range(5)
        ]
        scale = 1.0 / FOUR_PI
        out_ref[0:1, at] = scale * (jnp.sum(pot, 0, keepdims=True) + near[0])
        for a in range(3):
            whole = jnp.sum(y[a] * total[0] - 0.5 * total[1 + a], 0, keepdims=True)
            out_ref[1 + a : 2 + a, at] = -scale * (whole + (xrel[a : a + 1, at] * near[1] - near[2 + a]))

    uexp0[...] = mm(dens, hot[0])

    def far_pair(i, carry):
        uexp1[...] = mm(dens, hot[2 * i + 1])
        for h in range(2):
            far_tile(4 * i + h, uexp0, slice(128 * h, 128 * h + 128))
        uexp0[...] = mm(dens, hot[jnp.minimum(2 * i + 2, 7)])
        for h in range(2):
            far_tile(4 * i + 2 + h, uexp1, slice(128 * h, 128 * h + 128))
        return carry

    lax.fori_loop(0, 4, far_pair, 0)


def run(remote, *args):
    vmem = pl.BlockSpec(memory_space=pltpu.VMEM)
    smem = pl.BlockSpec(memory_space=pltpu.SMEM)
    anys = pl.BlockSpec(memory_space=pl.ANY)
    constants = [jnp.asarray(value) for value in tables()]
    dma = pltpu.SemaphoreType.DMA
    return pl.pallas_call(
        functools.partial(kernel, remote),
        out_shape=jax.ShapeDtypeStruct((4, 2048), F32),
        in_specs=([] if remote else [smem, vmem, vmem]) + [anys] * 16,
        out_specs=vmem,
        scratch_shapes=[
            pltpu.SMEM((512,), jnp.int32),
            pltpu.SMEM((64,), jnp.int32),
            pltpu.SMEM((64,), jnp.int32),
            pltpu.SMEM((1,), jnp.int32),
            pltpu.VMEM((1, 64), jnp.int32),
            pltpu.VMEM((1, 64), jnp.int32),
            pltpu.VMEM((1, NPTS), F32),
            pltpu.VMEM((4, 1024), F32),
            pltpu.VMEM((3, 2048), F32),
            pltpu.VMEM((8, NPTS), F32),
            pltpu.VMEM((64, NPTS), F32),
            pltpu.VMEM((WID, NPTS), F32),
            pltpu.VMEM((WID, 2 * WID), BF16),
            pltpu.VMEM((WID, WID), BF16),
            pltpu.VMEM((WID, WID), BF16),
            pltpu.VMEM((4, BLK, 128), F32),
            dma((16,)),
            pltpu.VMEM((8, 8, 128), F32),
            pltpu.VMEM((8, 8, 128), F32),
            pltpu.VMEM((8, 8, 128), F32),
            pltpu.VMEM((3, 4, 1024), F32),
            dma((7,)),
            dma((7,)),
            dma((7,)),
            dma((7,)),
            dma((2,)),
            dma((2,)),
            pltpu.VMEM((WID, 2 * WID), BF16),
            pltpu.VMEM((WID, 2 * WID), BF16),
            pltpu.VMEM((128, WID), F32),
            pltpu.VMEM((WID, 128), F32),
            pltpu.VMEM((WID, 128), F32),
            pltpu.VMEM((8, 128, 256), BF16),
            pltpu.VMEM((8, 2048), F32),
            pltpu.VMEM((32, 2048), F32),
            pltpu.VMEM((16, 32, 128), BF16),
            pltpu.VMEM((128, 1024), F32),
            pltpu.VMEM((24, 128, 128), BF16),
            pltpu.VMEM((24, 4, 128, 128), F32),
            pltpu.VMEM((512, 640), F32),
            pltpu.VMEM((16, 640), F32),
            pltpu.VMEM((WID, 256), F32),
            pltpu.VMEM((WID, 256), F32),
            pltpu.VMEM((UNROLL // 2, 128, 256), F32),
            pltpu.VMEM((UNROLL // 2, 128, 256), F32),
        ],
        compiler_params=pltpu.CompilerParams(
            vmem_limit_bytes=56 * 1024 * 1024, **(dict(collective_id=0, has_side_effects=True) if remote else {})
        ),
        name="downward",
    )(*args, *constants)


def per_device(
    coarse_dens, owner_slot, check_to_equiv, parent_own, leaf_own, leaf_counts, particles, panels, near_part,
    near_pan, near_count,
):
    return run(
        True, owner_slot, near_part, near_pan, near_count, near_part.reshape(1, 64), leaf_counts, coarse_dens.T, panels,
        particles, parent_own.T, leaf_own.T, check_to_equiv,
    )


def solution(mesh):
    both = ("grp", "box")
    placed = (
        P(None, both), P(), P(), P(None, both), P(None, both), P(both, None), P(None, both), P(None, both), P(both),
        P(both), P(both),
    )
    return jax.shard_map(per_device, mesh=mesh, in_specs=placed, out_specs=P(None, both), check_vma=False)
```

```python
import functools
import math

import jax
import jax.numpy as jnp
import ml_dtypes
import numpy as np
from jax import lax
from jax.experimental import pallas as pl
from jax.experimental.pallas import tpu as pltpu
from jax.sharding import PartitionSpec as P

ORDER = 12
EQUIV_RADIUS = 2.95
CHECK_RADIUS = 1.05
SOFTEN_SQ = 0.0625
FOUR_PI = 4.0 * math.pi
MESH = pl.DeviceIdType.MESH

NPTS = 728
MAGS = 91
BLK = 96
WID = 8 * BLK
F32, BF16 = jnp.float32, jnp.bfloat16


def surface_points(edge_points):
    spacing = np.linspace(-1.0, 1.0, edge_points)
    lattice = np.stack(np.meshgrid(spacing, spacing, spacing, indexing="ij"), 0).reshape(3, -1)
    on_surface = np.max(np.abs(lattice), axis=0) > 0.999
    return lattice[:, on_surface].astype(np.float32)


def split2(value):
    hi = value.astype(ml_dtypes.bfloat16)
    lo = (value - hi.astype(np.float32)).astype(ml_dtypes.bfloat16)
    return hi, lo


@functools.lru_cache(maxsize=None)
def tables():
    points = surface_points(ORDER).astype(np.float64)
    grid = np.rint((points + 1.0) * (ORDER - 1) / 2.0).astype(int)
    index = {tuple(g): i for i, g in enumerate(grid.T)}
    half = ORDER // 2
    mags = [g for g in grid.T if min(g) >= half]
    order = np.full(WID, -1)
    for s in range(8):
        for m, g in enumerate(mags):
            key = tuple(g[a] if s >> a & 1 else ORDER - 1 - g[a] for a in range(3))
            order[BLK * s + m] = index[key]
    live = order >= 0
    placed = points[:, np.where(live, order, 0)]
    targets = -0.5 + 0.5 * CHECK_RADIUS * placed
    separation = targets[:, :, None] - EQUIV_RADIUS * placed[:, None, :]
    k0 = 1.0 / (FOUR_PI * np.sqrt(np.sum(separation * separation, 0)))
    k0 = np.where(live[:, None] & live[None, :], k0, 0.0).astype(np.float32)
    k_pair = np.concatenate(split2(k0), 1)
    perm = np.zeros((WID, WID), np.float32)
    perm[np.nonzero(live)[0], order[live]] = 1.0
    size = np.ones((3, BLK))
    size[:, :MAGS] = np.array([[points[a, index[tuple(g)]] for g in mags] for a in range(3)])
    rows = np.concatenate([2.0 * EQUIV_RADIUS * size, EQUIV_RADIUS**2 * np.sum(size * size, 0)[None]], 0)
    mag = np.broadcast_to(rows.astype(np.float32)[:, :, None], (4, BLK, 128)).copy()
    return k_pair, perm.astype(ml_dtypes.bfloat16), perm.T.copy().astype(ml_dtypes.bfloat16), mag


def pieces3(value):
    hi = value.astype(BF16).astype(F32)
    rest = value - hi
    mid = rest.astype(BF16).astype(F32)
    return hi, mid, (rest - mid).astype(BF16).astype(F32)


def mm(a, b):
    return jnp.dot(a, b, preferred_element_type=F32)


UNROLL = 8


def kernel(
    remote, *refs,
):
    if not remote:
        device_ref, coarse_in, win_in, *refs = refs
    (
        owner_hbm, part_hbm, pan_hbm, count_ref, tile_hbm, counts_hbm, coarse_hbm, panels_hbm, parts_hbm, pown_hbm, lown_hbm,
        m_hbm, k_hbm, perm_hbm, permt_hbm, mag_hbm, out_ref,
        owner_ref, part_s, pan_s, tile_ref, counts_ref, parts_ref, pown_ref, lown_ref, m_ref, k_ref, perm_ref, permt_ref, mag_ref, load_sem,
        line, picked, crossed, win, relay, got, send1, recv1, send2, recv2, send3, recv3, send4, recv4,
        m_half, m_pair, turn, pown, lown, hot, xrel, xf, xk, pf, pk, zb, slots, acc, uexp0, uexp1, sq0, sq1,
    ) = refs
    if remote:
        grp, box = lax.axis_index("grp"), lax.axis_index("box")
        row, col = box // 8, box % 8
        me = grp * 64 + box
        early = box < 32
        late = box >= 32
        nxt, prv = lax.rem(me + 1, 512), lax.rem(me + 511, 512)
        cols = [row * 8 + lax.rem(col + r, 8) for r in range(1, 8)]
        along, side = row % 4, row // 4
        near_rows = [(side * 4 + lax.rem(along + r, 4)) * 8 + col for r in range(1, 4)]
        far_rows = [((1 - side) * 4 + lax.rem(along + r, 4)) * 8 + col for r in range(4)]
        rows = near_rows + far_rows
        beside = [(nxt // 64, nxt % 64), (prv // 64, prv % 64)]
        there = [me < 511, me > 0]
        turned_back = jnp.logical_and(col == 0, box != 32)
        greet = [
            jnp.logical_and(there[0], jnp.logical_or(col != 7, box == 31)),
            jnp.logical_and(there[1], box != 32),
        ]
        hear = [jnp.logical_and(there[0], box != 31), jnp.logical_and(there[1], jnp.logical_not(turned_back))]
        answer = [box == 31, jnp.logical_and(there[1], turned_back)]
        plain = jnp.logical_and(early, jnp.logical_and(box != 0, box != 31))
        barrier = pltpu.get_barrier_semaphore()

        @pl.when(early)
        def _():
            for other in near_rows + cols + far_rows:
                pl.semaphore_signal(barrier, inc=1, device_id=(grp, other), device_id_type=MESH)

        for r in range(2):

            @pl.when(greet[r])
            def _(r=r):
                pl.semaphore_signal(barrier, inc=1, device_id=beside[r], device_id_type=MESH)

        device = me
    else:
        row = 0
        device = device_ref[0]
    moves = {
        "coarse": (coarse_hbm, line.at[row]), "panels": (panels_hbm, win.at[1]), "owner": (owner_hbm, owner_ref),
        "counts": (counts_hbm, counts_ref), "parts": (parts_hbm, parts_ref), "part": (part_hbm, part_s),
        "pan": (pan_hbm, pan_s), "tile": (tile_hbm, tile_ref), "pown": (pown_hbm, pown_ref), "lown": (lown_hbm, lown_ref), "m": (m_hbm, m_ref.at[0:NPTS]),
        "permt": (permt_hbm, permt_ref), "perm": (perm_hbm, perm_ref), "k": (k_hbm, k_ref), "mag": (mag_hbm, mag_ref),
    }
    loads = {
        name: pltpu.make_async_copy(src, dst, load_sem.at[i]) for i, (name, (src, dst)) in enumerate(moves.items())
    }
    for load in loads.values():
        load.start()
    if remote:
        first = [
            pltpu.make_async_remote_copy(
                src_ref=coarse_hbm, dst_ref=line.at[row], send_sem=send1.at[r], recv_sem=recv1.at[r],
                device_id=(grp, rows[r]), device_id_type=MESH,
            )
            for r in range(7)
        ]
        second = [
            pltpu.make_async_remote_copy(
                src_ref=picked.at[r], dst_ref=crossed.at[col], send_sem=send2.at[r], recv_sem=recv2.at[r],
                device_id=(grp, cols[r]), device_id_type=MESH,
            )
            for r in range(7)
        ]
        third = pltpu.make_async_remote_copy(
            src_ref=relay, dst_ref=got, send_sem=send4.at[0], recv_sem=recv4.at[0],
            device_id=(grp, far_rows[0]), device_id_type=MESH,
        )
        halo = [
            pltpu.make_async_remote_copy(
                src_ref=panels_hbm, dst_ref=win.at[2 * r], send_sem=send3.at[r], recv_sem=recv3.at[r],
                device_id=beside[r], device_id_type=MESH,
            )
            for r in range(2)
        ]

    lane = lax.broadcasted_iota(jnp.int32, (1, 128), 1)

    axis = lax.broadcasted_iota(jnp.int32, (4, 1), 0)
    shift = jnp.zeros((4, 1), jnp.int32)
    for b in range(3):
        bit = jnp.bitwise_and(jnp.right_shift(device, 3 * b + axis), 1)
        shift = shift + jnp.left_shift(bit, b)
    centre = jnp.where(axis < 3, (8 * shift + 4).astype(F32), 0.0)

    def panel_part(s):
        raw = win[s] - centre
        z = raw[0:3]
        hi, mid, low = pieces3(z)
        for r, piece in enumerate((hi, hi, mid, hi, low, mid)):
            pf[3 * r : 3 * r + 3, :] = -2.0 * piece
        pf[18:21, :] = jnp.ones((3, 1024), F32)
        for r, piece in enumerate(pieces3(jnp.sum(z * z, 0, keepdims=True) + SOFTEN_SQ)):
            pf[21 + r : 22 + r, :] = piece
        pf[24:28, :] = raw

        for t in range(8):
            turned = pf[:, 128 * t : 128 * t + 128].T
            operand = turned[:, 0:32].astype(BF16)
            pk[8 * s + t] = jnp.zeros((128, 128), BF16)
            pk[8 * s + t, :, 0:32] = operand
            pk[8 * s + t, :, 64:96] = operand
            for a in range(4):
                zb[8 * s + t, a] = jnp.broadcast_to(turned[:, 24 + a : 25 + a], (128, 128))

    def prepare():
        loads["counts"].wait()
        counts = counts_ref[...].astype(F32)
        g_row = lax.broadcasted_iota(jnp.int32, (64, 64), 0)
        g_col = lax.broadcasted_iota(jnp.int32, (64, 64), 1)
        upto = jnp.sum(jnp.where(g_col <= g_row, counts, 0.0), 1, keepdims=True)
        before = jnp.sum(jnp.where(g_col < g_row, counts, 0.0), 1, keepdims=True)
        leaf = lax.broadcasted_iota(jnp.int32, (64, 1), 0)
        local = []
        for a in range(3):
            c = jnp.bitwise_and(jnp.right_shift(leaf, a), 1) + 2 * jnp.bitwise_and(jnp.right_shift(leaf, 3 + a), 1)
            local.append((2 * c - 3).astype(F32))
        loads["parts"].wait()
        for n in range(16):
            index = (lax.broadcasted_iota(jnp.int32, (1, 128), 1) + 128 * n).astype(F32)
            inside = jnp.where((index >= before) & (index < upto), 1.0, 0.0)
            side = slice(128 * (n % 2), 128 * (n % 2) + 128)
            hot[n // 2, 0:64, side] = inside.astype(BF16)
            hot[n // 2, 64:128, side] = inside.astype(BF16)
            for a in range(3):
                centre = jnp.sum(inside * local[a], 0, keepdims=True)
                xrel[a : a + 1, 128 * n : 128 * n + 128] = parts_ref[a : a + 1, 128 * n : 128 * n + 128] + centre

        xf[...] = jnp.zeros_like(xf)
        x = xrel[0:3, :]
        hi, mid, low = pieces3(x)
        for r, piece in enumerate((hi, mid, hi, low, hi, mid)):
            xf[3 * r : 3 * r + 3, :] = piece
        for r, piece in enumerate(pieces3(jnp.sum(x * x, 0, keepdims=True))):
            xf[18 + r : 19 + r, :] = piece
        xf[21:24, :] = jnp.ones((3, 2048), F32)
        for n in range(16):
            xk[n] = xf[:, 128 * n : 128 * n + 128].astype(BF16)
        pf[28:128, :] = jnp.zeros((100, 1024), F32)
        loads["panels"].wait()
        panel_part(1)

        loads["perm"].wait()

        def placed_own():
            value = turn[...]
            hi = value.astype(BF16).astype(F32)
            both = jnp.where(lax.broadcasted_iota(jnp.int32, (128, 1), 0) < 64, hi, value - hi).astype(BF16)
            product = lax.dot_general(perm_ref[...], both, (((1,), (1,)), ((), ())), preferred_element_type=F32)
            return product + pltpu.roll(product, 64, 1)

        turn[:, 640:WID] = jnp.zeros((128, 128), F32)
        loads["pown"].wait()
        for k in range(8):
            value = jnp.broadcast_to(pown_ref[k : k + 1, :], (8, NPTS))
            turn[8 * k : 8 * k + 8, 0:NPTS] = value
            turn[64 + 8 * k : 72 + 8 * k, 0:NPTS] = value
        pown[...] = placed_own()
        loads["lown"].wait()
        turn[0:64, 0:NPTS] = lown_ref[...]
        turn[64:128, 0:NPTS] = lown_ref[...]
        lown[...] = placed_own()


    def prepare_m():
        m_ref[NPTS:WID] = jnp.zeros((WID - NPTS, NPTS), F32)
        loads["m"].wait()
        loads["permt"].wait()
        m_half[:, 640:WID] = jnp.zeros((WID, 128), BF16)
        m_half[:, WID + 640 : 2 * WID] = jnp.zeros((WID, 128), BF16)

        def m_split(r, carry):
            at = pl.ds(pl.multiple_of(r * 64, 64), 64)
            value = m_ref[at, :]
            hi = value.astype(BF16)
            m_half[at, 0:NPTS] = hi
            m_half[at, WID : WID + NPTS] = (value - hi.astype(F32)).astype(BF16)
            return carry

        lax.fori_loop(0, 12, m_split, 0)

        def m_columns(r, carry):
            at = pl.ds(pl.multiple_of(r * 256, 256), 256)
            for side in (slice(0, WID), slice(WID, 2 * WID)):
                m_half[at, side] = mm(m_half[at, side], permt_ref[...]).astype(BF16)
            return carry

        lax.fori_loop(0, 3, m_columns, 0)

        def m_rows(r, carry):
            at = pl.ds(pl.multiple_of(r * 256, 256), 256)
            m_pair[:, at] = mm(perm_ref[...], m_half[:, at]).astype(BF16)
            return carry

        lax.fori_loop(0, 6, m_rows, 0)


    def window():
        if remote:
            pl.when(there[1])(halo[0].wait_recv)
            pl.when(answer[1])(halo[1].start)
            pl.when(jnp.logical_and(there[0], jnp.logical_not(answer[0])))(halo[1].wait_recv)

            @pl.when(jnp.logical_not(there[1]))
            def _():
                win[0] = jnp.zeros((4, 1024), F32)

            @pl.when(jnp.logical_not(there[0]))
            def _():
                win[2] = jnp.zeros((4, 1024), F32)

        panel_part(0)
        panel_part(2)

    if remote:
        pl.when(early)(prepare)
        heard = 4 + 6 * early.astype(jnp.int32) + hear[0].astype(jnp.int32) + hear[1].astype(jnp.int32)
        pl.semaphore_wait(barrier, heard)

        @pl.when(late)
        def _():
            for copy in first[3:]:
                copy.start()

        @pl.when(early)
        def _():
            for copy in first[:3]:
                copy.start()

        for r in range(2):
            pl.when(hear[r])(halo[r].start)
        pl.when(late)(prepare)
        prepare_m()
        loads["owner"].wait()
        loads["coarse"].wait()
        pl.when(plain)(window)

        @pl.when(answer[0])
        def _():
            halo[1].wait_recv()
            halo[0].start()

        @pl.when(early)
        def _():
            for copy in first:
                copy.wait_recv()
            for r in range(8):
                for h in range(2):
                    whose = (row + 4 * h) * 8 + lax.rem(col + r, 8)
                    want = jnp.bitwise_and(jnp.right_shift(owner_ref[grp * 64 + whose], 3), 7)
                    if r == 0:
                        crossed[col, h] = line[want]
                    else:
                        picked[r - 1, h] = line[want]
            for copy in second:
                copy.start()

        pl.when(jnp.logical_not(plain))(window)
    else:
        prepare()
        win[0] = win_in[0]
        win[2] = win_in[2]
        loads["owner"].wait()
        loads["coarse"].wait()
        prepare_m()
        window()

    loads["part"].wait()
    loads["pan"].wait()
    left = lax.broadcasted_iota(jnp.int32, (128, 128), 1) < 64
    blank = jnp.zeros((32, 128), BF16)

    def near_squares(i, into):
        for u in range(UNROLL // 2):
            t = i * UNROLL + 2 * u
            panel = jnp.where(left, pk[pan_s[t]], pk[pan_s[t + 1]])[:, 0:96]
            one, two = xk[part_s[t]], xk[part_s[t + 1]]
            part = jnp.concatenate(
                [jnp.concatenate([one, blank, blank], 0), jnp.concatenate([blank, blank, two], 0)], 1
            )
            into[u] = mm(panel, part)

    def near_sums(i, squares):
        for u in range(UNROLL):
            t = i * UNROLL + u
            tile = pan_s[t]
            side = slice(128 * (u % 2), 128 * (u % 2) + 128)
            sums = [jnp.zeros((8, 128), F32)] * 5
            for v in range(16):
                at = slice(8 * v, 8 * v + 8)
                inv = lax.rsqrt(squares[u // 2, at, side])
                w = zb[tile, 3, at] * inv
                w3 = w * (inv * inv)
                sums[0] = sums[0] + w
                sums[1] = sums[1] + w3
                for a in range(3):
                    sums[2 + a] = sums[2 + a] + w3 * zb[tile, a, at]
            at = pl.ds(pl.multiple_of(t * 8, 8), 8)
            for q in range(5):
                slots[at, 128 * q : 128 * q + 128] = sums[q]

    near_squares(0, sq0)
    steps = 64 // UNROLL

    def near_slots(i, carry):
        near_squares(2 * i + 1, sq1)
        near_sums(2 * i, sq0)
        near_squares(jnp.minimum(2 * i + 2, steps - 1), sq0)
        near_sums(2 * i + 1, sq1)
        return carry

    lax.fori_loop(0, steps // 2, near_slots, 0)
    loads["tile"].wait()
    slot = lax.broadcasted_iota(jnp.int32, (1, 64), 1)
    live = jnp.where(slot < count_ref[...], tile_ref[...], 31).astype(F32)
    e_row = lax.broadcasted_iota(jnp.int32, (64, 512), 0)
    e_col = lax.broadcasted_iota(jnp.int32, (64, 512), 1)
    spread8 = jnp.where(jnp.right_shift(e_col, 3) == e_row, 1.0, 0.0).astype(BF16)
    target = mm(jnp.broadcast_to(live, (16, 64)).astype(BF16), spread8)
    n_row = lax.broadcasted_iota(jnp.int32, (16, 512), 0).astype(F32)
    choose = jnp.where(target == n_row, 1.0, 0.0).astype(BF16)
    hi, mid, low = pieces3(slots[...])
    acc[...] = mm(choose, hi.astype(BF16)) + (mm(choose, mid.astype(BF16)) + mm(choose, low.astype(BF16)))

    low_half = lane < 64
    column = jnp.bitwise_and(lane, 63)

    def swapped(value, octant):
        blocks = [value[BLK * s : BLK * s + BLK] for s in range(8)]
        for b in range(3):
            mask = jnp.bitwise_and(jnp.right_shift(octant, b), 1) == 1
            blocks = [jnp.where(mask, blocks[s ^ (1 << b)], blocks[s]) for s in range(8)]
        return jnp.concatenate(blocks, 0)

    def pieces(value):
        hi = value.astype(BF16).astype(F32)
        return jnp.where(low_half, hi, value - hi).astype(BF16)

    def both(pair_ref, x2):
        product = mm(pair_ref[...], jnp.concatenate([x2, x2], 0))
        return product + pltpu.roll(product, 64, 1)

    def level(x2, octant, own):
        checks = swapped(pieces(both(k_ref, swapped(x2, octant))), octant)
        return both(m_pair, checks) + own

    loads["k"].wait()
    loads["mag"].wait()
    if remote:

        @pl.when(early)
        def _():
            for copy in second:
                copy.wait_recv()
            got[...] = crossed[jnp.bitwise_and(owner_ref[me], 7), 0]
            relay[...] = crossed[jnp.bitwise_and(owner_ref[me + 32], 7), 1]
            third.start()

        pl.when(late)(third.wait_recv)
        coarse = got[...]
    else:
        coarse = coarse_in[...]
    half = lax.broadcasted_iota(jnp.int32, (128, 1), 0) < 64
    hi = coarse.astype(BF16).astype(F32)
    turn[:, 0:NPTS] = jnp.where(half, hi, coarse - hi)
    spread = turn[...].astype(BF16)
    start = lax.dot_general(perm_ref[...], spread, (((1,), (1,)), ((), ())), preferred_element_type=F32)
    parents = level(start.astype(BF16), jnp.right_shift(column, 3), pown[...])
    leaves = level(pieces(parents), jnp.bitwise_and(column, 7), lown[...])
    dens = pieces(leaves)

    def far_tile(n, dense, side):
        at = pl.ds(pl.multiple_of(n * 128, 128), 128)
        y = [jnp.broadcast_to(parts_ref[a : a + 1, at], (8, 128)) for a in range(3)]
        y2 = y[0] * y[0] + y[1] * y[1] + y[2] * y[2]
        pot = jnp.zeros((8, 128), F32)
        total = [jnp.zeros((8, 128), F32)] * 4
        for v in range(BLK // 8):
            band = slice(8 * v, 8 * v + 8)
            mags = [mag_ref[a, band] for a in range(3)]
            part = [y2 + mag_ref[3, band]]
            for a in range(3):
                step = y[a] * mags[a]
                part = [q + step for q in part] + [q - step for q in part]
            w3 = []
            for s in range(8):
                inv = lax.rsqrt(part[s])
                w = dense[BLK * s + 8 * v : BLK * s + 8 * v + 8, side] * inv
                pot = pot + w
                w3.append(w * (inv * inv))
            x0 = [w3[s] + w3[s + 1] for s in (0, 2, 4, 6)]
            x1 = [w3[s + 1] - w3[s] for s in (0, 2, 4, 6)]
            y0 = [x0[s] + x0[s + 1] for s in (0, 2)]
            y1 = [x0[s + 1] - x0[s] for s in (0, 2)]
            total[0] = total[0] + (y0[0] + y0[1])
            total[1] = total[1] + ((x1[0] + x1[1]) + (x1[2] + x1[3])) * mags[0]
            total[2] = total[2] + (y1[0] + y1[1]) * mags[1]
            total[3] = total[3] + (y0[1] - y0[0]) * mags[2]
        mine = lax.broadcasted_iota(jnp.int32, (16, 128), 0) == n
        near = [
            jnp.sum(jnp.where(mine, acc[:, 128 * q : 128 * q + 128], 0.0), 0, keepdims=True) for q in range(5)
        ]
        scale = 1.0 / FOUR_PI
        out_ref[0:1, at] = scale * (jnp.sum(pot, 0, keepdims=True) + near[0])
        for a in range(3):
            whole = jnp.sum(y[a] * total[0] - 0.5 * total[1 + a], 0, keepdims=True)
            out_ref[1 + a : 2 + a, at] = -scale * (whole + (xrel[a : a + 1, at] * near[1] - near[2 + a]))

    uexp0[...] = mm(dens, hot[0])

    def far_pair(i, carry):
        uexp1[...] = mm(dens, hot[2 * i + 1])
        for h in range(2):
            far_tile(4 * i + h, uexp0, slice(128 * h, 128 * h + 128))
        uexp0[...] = mm(dens, hot[jnp.minimum(2 * i + 2, 7)])
        for h in range(2):
            far_tile(4 * i + 2 + h, uexp1, slice(128 * h, 128 * h + 128))
        return carry

    lax.fori_loop(0, 4, far_pair, 0)
    if remote:
        for r in range(2):
            pl.when(there[r])(halo[r].wait_send)

        @pl.when(early)
        def _():
            for copy in first[:3] + second + [third]:
                copy.wait_send()

        @pl.when(late)
        def _():
            for copy in first[3:]:
                copy.wait_send()


def run(remote, *args):
    vmem = pl.BlockSpec(memory_space=pltpu.VMEM)
    smem = pl.BlockSpec(memory_space=pltpu.SMEM)
    anys = pl.BlockSpec(memory_space=pl.ANY)
    constants = [jnp.asarray(value) for value in tables()]
    dma = pltpu.SemaphoreType.DMA
    return pl.pallas_call(
        functools.partial(kernel, remote),
        out_shape=jax.ShapeDtypeStruct((4, 2048), F32),
        in_specs=([] if remote else [smem, vmem, vmem]) + [anys] * 3 + [vmem] + [anys] * 12,
        out_specs=vmem,
        scratch_shapes=[
            pltpu.SMEM((512,), jnp.int32),
            pltpu.SMEM((64,), jnp.int32),
            pltpu.SMEM((64,), jnp.int32),
            pltpu.VMEM((1, 64), jnp.int32),
            pltpu.VMEM((1, 64), jnp.int32),
            pltpu.VMEM((3, 2048), F32),
            pltpu.VMEM((8, NPTS), F32),
            pltpu.VMEM((64, NPTS), F32),
            pltpu.VMEM((WID, NPTS), F32),
            pltpu.VMEM((WID, 2 * WID), BF16),
            pltpu.VMEM((WID, WID), BF16),
            pltpu.VMEM((WID, WID), BF16),
            pltpu.VMEM((4, BLK, 128), F32),
            dma((15,)),
            pltpu.VMEM((8, 1, NPTS), F32),
            pltpu.VMEM((7, 2, 1, NPTS), F32),
            pltpu.VMEM((8, 2, 1, NPTS), F32),
            pltpu.VMEM((3, 4, 1024), F32),
            pltpu.VMEM((1, NPTS), F32),
            pltpu.VMEM((1, NPTS), F32),
            dma((7,)),
            dma((7,)),
            dma((7,)),
            dma((7,)),
            dma((2,)),
            dma((2,)),
            dma((1,)),
            dma((1,)),
            pltpu.VMEM((WID, 2 * WID), BF16),
            pltpu.VMEM((WID, 2 * WID), BF16),
            pltpu.VMEM((128, WID), F32),
            pltpu.VMEM((WID, 128), F32),
            pltpu.VMEM((WID, 128), F32),
            pltpu.VMEM((8, 128, 256), BF16),
            pltpu.VMEM((8, 2048), F32),
            pltpu.VMEM((32, 2048), F32),
            pltpu.VMEM((16, 32, 128), BF16),
            pltpu.VMEM((128, 1024), F32),
            pltpu.VMEM((24, 128, 128), BF16),
            pltpu.VMEM((24, 4, 128, 128), F32),
            pltpu.VMEM((512, 640), F32),
            pltpu.VMEM((16, 640), F32),
            pltpu.VMEM((WID, 256), F32),
            pltpu.VMEM((WID, 256), F32),
            pltpu.VMEM((UNROLL // 2, 128, 256), F32),
            pltpu.VMEM((UNROLL // 2, 128, 256), F32),
        ],
        compiler_params=pltpu.CompilerParams(
            vmem_limit_bytes=56 * 1024 * 1024, **(dict(collective_id=0, has_side_effects=True) if remote else {})
        ),
        name="downward",
    )(*args, *constants)


def per_device(
    coarse_dens, owner_slot, check_to_equiv, parent_own, leaf_own, leaf_counts, particles, panels, near_part,
    near_pan, near_count,
):
    return run(
        True, owner_slot, near_part, near_pan, near_count.reshape(1, 1), near_part.reshape(1, 64), leaf_counts, coarse_dens.T, panels,
        particles, parent_own.T, leaf_own.T, check_to_equiv,
    )


def solution(mesh):
    both = ("grp", "box")
    placed = (
        P(None, both), P(), P(), P(None, both), P(None, both), P(both, None), P(None, both), P(None, both), P(both),
        P(both), P(both),
    )
    return jax.shard_map(per_device, mesh=mesh, in_specs=placed, out_specs=P(None, both), check_vma=False)
```

```python
import functools
import math

import jax
import jax.numpy as jnp
import ml_dtypes
import numpy as np
from jax import lax
from jax.experimental import pallas as pl
from jax.experimental.pallas import tpu as pltpu
from jax.sharding import PartitionSpec as P

ORDER = 12
EQUIV_RADIUS = 2.95
CHECK_RADIUS = 1.05
SOFTEN_SQ = 0.0625
FOUR_PI = 4.0 * math.pi
MESH = pl.DeviceIdType.MESH

NPTS = 728
MAGS = 91
BLK = 96
WID = 8 * BLK
F32, BF16 = jnp.float32, jnp.bfloat16


def surface_points(edge_points):
    spacing = np.linspace(-1.0, 1.0, edge_points)
    lattice = np.stack(np.meshgrid(spacing, spacing, spacing, indexing="ij"), 0).reshape(3, -1)
    on_surface = np.max(np.abs(lattice), axis=0) > 0.999
    return lattice[:, on_surface].astype(np.float32)


def split2(value):
    hi = value.astype(ml_dtypes.bfloat16)
    lo = (value - hi.astype(np.float32)).astype(ml_dtypes.bfloat16)
    return hi, lo


@functools.lru_cache(maxsize=None)
def tables():
    points = surface_points(ORDER).astype(np.float64)
    grid = np.rint((points + 1.0) * (ORDER - 1) / 2.0).astype(int)
    index = {tuple(g): i for i, g in enumerate(grid.T)}
    half = ORDER // 2
    mags = [g for g in grid.T if min(g) >= half]
    order = np.full(WID, -1)
    for s in range(8):
        for m, g in enumerate(mags):
            key = tuple(g[a] if s >> a & 1 else ORDER - 1 - g[a] for a in range(3))
            order[BLK * s + m] = index[key]
    live = order >= 0
    placed = points[:, np.where(live, order, 0)]
    targets = -0.5 + 0.5 * CHECK_RADIUS * placed
    separation = targets[:, :, None] - EQUIV_RADIUS * placed[:, None, :]
    k0 = 1.0 / (FOUR_PI * np.sqrt(np.sum(separation * separation, 0)))
    k0 = np.where(live[:, None] & live[None, :], k0, 0.0).astype(np.float32)
    k_pair = np.concatenate(split2(k0), 1)
    perm = np.zeros((WID, WID), np.float32)
    perm[np.nonzero(live)[0], order[live]] = 1.0
    size = np.ones((3, BLK))
    size[:, :MAGS] = np.array([[points[a, index[tuple(g)]] for g in mags] for a in range(3)])
    rows = np.concatenate([2.0 * EQUIV_RADIUS * size, EQUIV_RADIUS**2 * np.sum(size * size, 0)[None]], 0)
    mag = np.broadcast_to(rows.astype(np.float32)[:, :, None], (4, BLK, 128)).copy()
    return k_pair, perm.astype(ml_dtypes.bfloat16), perm.T.copy().astype(ml_dtypes.bfloat16), mag


def pieces3(value):
    hi = value.astype(BF16).astype(F32)
    rest = value - hi
    mid = rest.astype(BF16).astype(F32)
    return hi, mid, (rest - mid).astype(BF16).astype(F32)


def mm(a, b):
    return jnp.dot(a, b, preferred_element_type=F32)


UNROLL = 8


def kernel(
    remote, *refs,
):
    if not remote:
        device_ref, coarse_in, win_in, *refs = refs
    (
        owner_hbm, part_hbm, pan_hbm, count_ref, tile_hbm, counts_hbm, coarse_hbm, panels_hbm, parts_hbm, pown_hbm, lown_hbm,
        m_hbm, k_hbm, perm_hbm, permt_hbm, mag_hbm, out_ref,
        owner_ref, part_s, pan_s, tile_ref, counts_ref, parts_ref, pown_ref, lown_ref, m_ref, k_ref, perm_ref, permt_ref, mag_ref, load_sem,
        line, picked, crossed, win, relay, got, send1, recv1, send2, recv2, send3, recv3, send4, recv4, extra, send5, recv5,
        m_half, m_pair, turn, pown, lown, hot, xrel, xf, xk, pf, pk, zb, slots, acc, uexp0, uexp1, sq0, sq1, inv_one, inv_cube,
    ) = refs
    if remote:
        grp, box = lax.axis_index("grp"), lax.axis_index("box")
        row, col = box // 8, box % 8
        me = grp * 64 + box
        early = box < 32
        late = box >= 32
        nxt, prv = lax.rem(me + 1, 512), lax.rem(me + 511, 512)
        cols = [row * 8 + lax.rem(col + r, 8) for r in range(1, 8)]
        along, side = row % 4, row // 4
        near_rows = [(side * 4 + lax.rem(along + r, 4)) * 8 + col for r in range(1, 4)]
        far_rows = [((1 - side) * 4 + lax.rem(along + r, 4)) * 8 + col for r in range(4)]
        rows = near_rows + far_rows
        beside = [(nxt // 64, nxt % 64), (prv // 64, prv % 64)]
        there = [me < 511, me > 0]
        turned_back = jnp.logical_and(col == 0, jnp.logical_or(box == 0, box > 32))
        greet = [
            jnp.logical_and(there[0], jnp.logical_or(col != 7, box <= 31)),
            jnp.logical_and(there[1], box != 32),
        ]
        hear = [jnp.logical_and(there[0], box != 31), jnp.logical_and(there[1], jnp.logical_not(turned_back))]
        answer = jnp.logical_and(there[1], turned_back)
        plain = jnp.logical_and(early, jnp.logical_and(box != 0, col < 4))
        barrier = pltpu.get_barrier_semaphore()

        @pl.when(early)
        def _():
            for other in near_rows + cols + far_rows:
                pl.semaphore_signal(barrier, inc=1, device_id=(grp, other), device_id_type=MESH)

        @pl.when(box == 0)
        def _():
            pl.semaphore_signal(barrier, inc=1, device_id=(grp, 31), device_id_type=MESH)

        @pl.when(box == 31)
        def _():
            pl.semaphore_signal(barrier, inc=1, device_id=(grp, 0), device_id_type=MESH)

        for r in range(2):

            @pl.when(greet[r])
            def _(r=r):
                pl.semaphore_signal(barrier, inc=1, device_id=beside[r], device_id_type=MESH)

        device = me
    else:
        row = 0
        device = device_ref[0]
    moves = {
        "coarse": (coarse_hbm, line.at[row]), "panels": (panels_hbm, win.at[1]), "owner": (owner_hbm, owner_ref),
        "counts": (counts_hbm, counts_ref), "parts": (parts_hbm, parts_ref), "part": (part_hbm, part_s),
        "pan": (pan_hbm, pan_s), "tile": (tile_hbm, tile_ref), "pown": (pown_hbm, pown_ref), "lown": (lown_hbm, lown_ref), "m": (m_hbm, m_ref.at[0:NPTS]),
        "permt": (permt_hbm, permt_ref), "perm": (perm_hbm, perm_ref), "k": (k_hbm, k_ref), "mag": (mag_hbm, mag_ref),
    }
    loads = {
        name: pltpu.make_async_copy(src, dst, load_sem.at[i]) for i, (name, (src, dst)) in enumerate(moves.items())
    }
    for load in loads.values():
        load.start()
    if remote:
        first = [
            pltpu.make_async_remote_copy(
                src_ref=coarse_hbm, dst_ref=line.at[row], send_sem=send1.at[r], recv_sem=recv1.at[r],
                device_id=(grp, rows[r]), device_id_type=MESH,
            )
            for r in range(7)
        ]
        second = [
            pltpu.make_async_remote_copy(
                src_ref=picked.at[r], dst_ref=crossed.at[col], send_sem=send2.at[r], recv_sem=recv2.at[r],
                device_id=(grp, cols[r]), device_id_type=MESH,
            )
            for r in range(7)
        ]
        third = pltpu.make_async_remote_copy(
            src_ref=relay, dst_ref=got, send_sem=send4.at[0], recv_sem=recv4.at[0],
            device_id=(grp, far_rows[0]), device_id_type=MESH,
        )
        lent = pltpu.make_async_remote_copy(
            src_ref=panels_hbm, dst_ref=extra, send_sem=send5.at[0], recv_sem=recv5.at[0],
            device_id=(grp, 0), device_id_type=MESH,
        )
        passed = pltpu.make_async_remote_copy(
            src_ref=extra, dst_ref=win.at[0], send_sem=send5.at[1], recv_sem=recv5.at[1],
            device_id=(grp, 32), device_id_type=MESH,
        )
        halo = [
            pltpu.make_async_remote_copy(
                src_ref=panels_hbm, dst_ref=win.at[2 * r], send_sem=send3.at[r], recv_sem=recv3.at[r],
                device_id=beside[r], device_id_type=MESH,
            )
            for r in range(2)
        ]

    lane = lax.broadcasted_iota(jnp.int32, (1, 128), 1)

    axis = lax.broadcasted_iota(jnp.int32, (4, 1), 0)
    shift = jnp.zeros((4, 1), jnp.int32)
    for b in range(3):
        bit = jnp.bitwise_and(jnp.right_shift(device, 3 * b + axis), 1)
        shift = shift + jnp.left_shift(bit, b)
    centre = jnp.where(axis < 3, (8 * shift + 4).astype(F32), 0.0)

    def panel_part(s):
        raw = win[s] - centre
        z = raw[0:3]
        hi, mid, low = pieces3(z)
        for r, piece in enumerate((hi, hi, mid, hi, low, mid)):
            pf[3 * r : 3 * r + 3, :] = -2.0 * piece
        pf[18:21, :] = jnp.ones((3, 1024), F32)
        for r, piece in enumerate(pieces3(jnp.sum(z * z, 0, keepdims=True) + SOFTEN_SQ)):
            pf[21 + r : 22 + r, :] = piece
        pf[24:28, :] = raw

        for t in range(8):
            turned = pf[:, 128 * t : 128 * t + 128].T
            operand = turned[:, 0:32].astype(BF16)
            pk[8 * s + t] = jnp.zeros((128, 128), BF16)
            pk[8 * s + t, :, 0:32] = operand
            pk[8 * s + t, :, 64:96] = operand
            for a in range(4):
                zb[8 * s + t, a] = jnp.broadcast_to(turned[:, 24 + a : 25 + a], (128, 128))

    def prepare():
        loads["counts"].wait()
        counts = counts_ref[...].astype(F32)
        g_row = lax.broadcasted_iota(jnp.int32, (64, 64), 0)
        g_col = lax.broadcasted_iota(jnp.int32, (64, 64), 1)
        upto = jnp.sum(jnp.where(g_col <= g_row, counts, 0.0), 1, keepdims=True)
        before = jnp.sum(jnp.where(g_col < g_row, counts, 0.0), 1, keepdims=True)
        leaf = lax.broadcasted_iota(jnp.int32, (64, 1), 0)
        local = []
        for a in range(3):
            c = jnp.bitwise_and(jnp.right_shift(leaf, a), 1) + 2 * jnp.bitwise_and(jnp.right_shift(leaf, 3 + a), 1)
            local.append((2 * c - 3).astype(F32))
        loads["parts"].wait()
        for n in range(16):
            index = (lax.broadcasted_iota(jnp.int32, (1, 128), 1) + 128 * n).astype(F32)
            inside = jnp.where((index >= before) & (index < upto), 1.0, 0.0)
            side = slice(128 * (n % 2), 128 * (n % 2) + 128)
            hot[n // 2, 0:64, side] = inside.astype(BF16)
            hot[n // 2, 64:128, side] = inside.astype(BF16)
            for a in range(3):
                centre = jnp.sum(inside * local[a], 0, keepdims=True)
                xrel[a : a + 1, 128 * n : 128 * n + 128] = parts_ref[a : a + 1, 128 * n : 128 * n + 128] + centre

        xf[...] = jnp.zeros_like(xf)
        x = xrel[0:3, :]
        hi, mid, low = pieces3(x)
        for r, piece in enumerate((hi, mid, hi, low, hi, mid)):
            xf[3 * r : 3 * r + 3, :] = piece
        for r, piece in enumerate(pieces3(jnp.sum(x * x, 0, keepdims=True))):
            xf[18 + r : 19 + r, :] = piece
        xf[21:24, :] = jnp.ones((3, 2048), F32)
        for n in range(16):
            xk[n] = xf[:, 128 * n : 128 * n + 128].astype(BF16)
        pf[28:128, :] = jnp.zeros((100, 1024), F32)
        loads["panels"].wait()
        panel_part(1)

        loads["perm"].wait()

        def placed_own():
            value = turn[...]
            hi = value.astype(BF16).astype(F32)
            both = jnp.where(lax.broadcasted_iota(jnp.int32, (128, 1), 0) < 64, hi, value - hi).astype(BF16)
            product = lax.dot_general(perm_ref[...], both, (((1,), (1,)), ((), ())), preferred_element_type=F32)
            return product + pltpu.roll(product, 64, 1)

        turn[:, 640:WID] = jnp.zeros((128, 128), F32)
        loads["pown"].wait()
        for k in range(8):
            value = jnp.broadcast_to(pown_ref[k : k + 1, :], (8, NPTS))
            turn[8 * k : 8 * k + 8, 0:NPTS] = value
            turn[64 + 8 * k : 72 + 8 * k, 0:NPTS] = value
        pown[...] = placed_own()
        loads["lown"].wait()
        turn[0:64, 0:NPTS] = lown_ref[...]
        turn[64:128, 0:NPTS] = lown_ref[...]
        lown[...] = placed_own()


    def prepare_m():
        m_ref[NPTS:WID] = jnp.zeros((WID - NPTS, NPTS), F32)
        loads["m"].wait()
        loads["permt"].wait()
        m_half[:, 640:WID] = jnp.zeros((WID, 128), BF16)
        m_half[:, WID + 640 : 2 * WID] = jnp.zeros((WID, 128), BF16)

        def m_split(r, carry):
            at = pl.ds(pl.multiple_of(r * 64, 64), 64)
            value = m_ref[at, :]
            hi = value.astype(BF16)
            m_half[at, 0:NPTS] = hi
            m_half[at, WID : WID + NPTS] = (value - hi.astype(F32)).astype(BF16)
            return carry

        lax.fori_loop(0, 12, m_split, 0)

        def m_columns(r, carry):
            at = pl.ds(pl.multiple_of(r * 256, 256), 256)
            for side in (slice(0, WID), slice(WID, 2 * WID)):
                m_half[at, side] = mm(m_half[at, side], permt_ref[...]).astype(BF16)
            return carry

        lax.fori_loop(0, 3, m_columns, 0)

        def m_rows(r, carry):
            at = pl.ds(pl.multiple_of(r * 256, 256), 256)
            m_pair[:, at] = mm(perm_ref[...], m_half[:, at]).astype(BF16)
            return carry

        lax.fori_loop(0, 6, m_rows, 0)


    def prepare_far():
        loads["mag"].wait()

        def distances(n, carry):
            at = pl.ds(pl.multiple_of(n * 128, 128), 128)
            y = [jnp.broadcast_to(parts_ref[a : a + 1, at], (8, 128)) for a in range(3)]
            y2 = y[0] * y[0] + y[1] * y[1] + y[2] * y[2]
            for v in range(BLK // 8):
                band = slice(8 * v, 8 * v + 8)
                part = [y2 + mag_ref[3, band]]
                for a in range(3):
                    step = y[a] * mag_ref[a, band]
                    part = [q + step for q in part] + [q - step for q in part]
                for s in range(8):
                    inv = lax.rsqrt(part[s])
                    inv_one[n, BLK * s + 8 * v : BLK * s + 8 * v + 8] = inv
                    inv_cube[n, BLK * s + 8 * v : BLK * s + 8 * v + 8] = inv * (inv * inv)
            return carry

        lax.fori_loop(0, 16, distances, 0)

    def window():
        if remote:
            pl.when(jnp.logical_and(there[1], jnp.logical_not(jnp.logical_or(answer, box == 32))))(halo[0].wait_recv)
            pl.when(there[0])(halo[1].wait_recv)
            pl.when(box == 32)(passed.wait_recv)

            @pl.when(jnp.logical_not(there[1]))
            def _():
                win[0] = jnp.zeros((4, 1024), F32)

            @pl.when(jnp.logical_not(there[0]))
            def _():
                win[2] = jnp.zeros((4, 1024), F32)

        panel_part(0)
        panel_part(2)

    if remote:
        pl.when(early)(prepare)
        heard = 4 + 6 * early.astype(jnp.int32) + hear[0].astype(jnp.int32) + hear[1].astype(jnp.int32)
        heard = heard + jnp.logical_or(box == 0, box == 31).astype(jnp.int32)
        pl.semaphore_wait(barrier, heard)
        pl.when(box == 31)(lent.start)

        @pl.when(late)
        def _():
            for copy in first[3:]:
                copy.start()

        @pl.when(early)
        def _():
            for copy in first[:3]:
                copy.start()

        for r in range(2):
            pl.when(hear[r])(halo[r].start)
        pl.when(late)(prepare)
        prepare_m()

        @pl.when(jnp.logical_and(answer, late))
        def _():
            halo[0].wait_recv()
            halo[1].start()

        pl.when(jnp.logical_or(late, col < 4))(prepare_far)
        loads["owner"].wait()
        loads["coarse"].wait()
        pl.when(plain)(window)

        @pl.when(early)
        def _():
            for copy in first:
                copy.wait_recv()

            @pl.when(box == 0)
            def _():
                lent.wait_recv()
                passed.start()

            for r in range(8):
                for h in range(2):
                    whose = (row + 4 * h) * 8 + lax.rem(col + r, 8)
                    want = jnp.bitwise_and(jnp.right_shift(owner_ref[grp * 64 + whose], 3), 7)
                    if r == 0:
                        crossed[col, h] = line[want]
                    else:
                        picked[r - 1, h] = line[want]
            for copy in second:
                copy.start()

        @pl.when(jnp.logical_and(answer, early))
        def _():
            halo[0].wait_recv()
            halo[1].start()

        pl.when(jnp.logical_not(plain))(window)
    else:
        prepare()
        win[0] = win_in[0]
        win[2] = win_in[2]
        loads["owner"].wait()
        loads["coarse"].wait()
        prepare_m()
        prepare_far()
        window()

    loads["part"].wait()
    loads["pan"].wait()
    left = lax.broadcasted_iota(jnp.int32, (128, 128), 1) < 64
    blank = jnp.zeros((32, 128), BF16)

    def near_squares(i, into):
        for u in range(UNROLL // 2):
            t = i * UNROLL + 2 * u
            panel = jnp.where(left, pk[pan_s[t]], pk[pan_s[t + 1]])[:, 0:96]
            one, two = xk[part_s[t]], xk[part_s[t + 1]]
            part = jnp.concatenate(
                [jnp.concatenate([one, blank, blank], 0), jnp.concatenate([blank, blank, two], 0)], 1
            )
            into[u] = mm(panel, part)

    def near_sums(i, squares):
        for u in range(UNROLL):
            t = i * UNROLL + u
            tile = pan_s[t]
            side = slice(128 * (u % 2), 128 * (u % 2) + 128)
            sums = [jnp.zeros((8, 128), F32)] * 5
            for v in range(16):
                at = slice(8 * v, 8 * v + 8)
                inv = lax.rsqrt(squares[u // 2, at, side])
                w = zb[tile, 3, at] * inv
                w3 = w * (inv * inv)
                sums[0] = sums[0] + w
                sums[1] = sums[1] + w3
                for a in range(3):
                    sums[2 + a] = sums[2 + a] + w3 * zb[tile, a, at]
            at = pl.ds(pl.multiple_of(t * 8, 8), 8)
            for q in range(5):
                slots[at, 128 * q : 128 * q + 128] = sums[q]

    near_squares(0, sq0)
    steps = 64 // UNROLL

    def near_slots(i, carry):
        near_squares(2 * i + 1, sq1)
        near_sums(2 * i, sq0)
        near_squares(jnp.minimum(2 * i + 2, steps - 1), sq0)
        near_sums(2 * i + 1, sq1)
        return carry

    lax.fori_loop(0, steps // 2, near_slots, 0)
    if remote:
        pl.when(jnp.logical_and(early, col >= 4))(prepare_far)
    loads["tile"].wait()
    slot = lax.broadcasted_iota(jnp.int32, (1, 64), 1)
    live = jnp.where(slot < count_ref[...], tile_ref[...], 31).astype(F32)
    e_row = lax.broadcasted_iota(jnp.int32, (64, 512), 0)
    e_col = lax.broadcasted_iota(jnp.int32, (64, 512), 1)
    spread8 = jnp.where(jnp.right_shift(e_col, 3) == e_row, 1.0, 0.0).astype(BF16)
    target = mm(jnp.broadcast_to(live, (16, 64)).astype(BF16), spread8)
    n_row = lax.broadcasted_iota(jnp.int32, (16, 512), 0).astype(F32)
    choose = jnp.where(target == n_row, 1.0, 0.0).astype(BF16)
    hi, mid, low = pieces3(slots[...])
    acc[...] = mm(choose, hi.astype(BF16)) + (mm(choose, mid.astype(BF16)) + mm(choose, low.astype(BF16)))

    low_half = lane < 64
    column = jnp.bitwise_and(lane, 63)

    def swapped(value, octant):
        blocks = [value[BLK * s : BLK * s + BLK] for s in range(8)]
        for b in range(3):
            mask = jnp.bitwise_and(jnp.right_shift(octant, b), 1) == 1
            blocks = [jnp.where(mask, blocks[s ^ (1 << b)], blocks[s]) for s in range(8)]
        return jnp.concatenate(blocks, 0)

    def pieces(value):
        hi = value.astype(BF16).astype(F32)
        return jnp.where(low_half, hi, value - hi).astype(BF16)

    def both(pair_ref, x2):
        product = mm(pair_ref[...], jnp.concatenate([x2, x2], 0))
        return product + pltpu.roll(product, 64, 1)

    def level(x2, octant, own):
        checks = swapped(pieces(both(k_ref, swapped(x2, octant))), octant)
        return both(m_pair, checks) + own

    loads["k"].wait()
    if remote:

        @pl.when(early)
        def _():
            for copy in second:
                copy.wait_recv()
            got[...] = crossed[jnp.bitwise_and(owner_ref[me], 7), 0]
            relay[...] = crossed[jnp.bitwise_and(owner_ref[me + 32], 7), 1]
            third.start()

        pl.when(late)(third.wait_recv)
        coarse = got[...]
    else:
        coarse = coarse_in[...]
    half = lax.broadcasted_iota(jnp.int32, (128, 1), 0) < 64
    hi = coarse.astype(BF16).astype(F32)
    turn[:, 0:NPTS] = jnp.where(half, hi, coarse - hi)
    spread = turn[...].astype(BF16)
    start = lax.dot_general(perm_ref[...], spread, (((1,), (1,)), ((), ())), preferred_element_type=F32)
    parents = level(start.astype(BF16), jnp.right_shift(column, 3), pown[...])
    leaves = level(pieces(parents), jnp.bitwise_and(column, 7), lown[...])
    dens = pieces(leaves)

    def far_tile(n, dense, side):
        at = pl.ds(pl.multiple_of(n * 128, 128), 128)
        y = [jnp.broadcast_to(parts_ref[a : a + 1, at], (8, 128)) for a in range(3)]
        pot = jnp.zeros((8, 128), F32)
        total = [jnp.zeros((8, 128), F32)] * 4
        for v in range(BLK // 8):
            band = slice(8 * v, 8 * v + 8)
            mags = [mag_ref[a, band] for a in range(3)]
            w3 = []
            for s in range(8):
                at8 = slice(BLK * s + 8 * v, BLK * s + 8 * v + 8)
                u = dense[at8, side]
                pot = pot + u * inv_one[n, at8]
                w3.append(u * inv_cube[n, at8])
            x0 = [w3[s] + w3[s + 1] for s in (0, 2, 4, 6)]
            x1 = [w3[s + 1] - w3[s] for s in (0, 2, 4, 6)]
            y0 = [x0[s] + x0[s + 1] for s in (0, 2)]
            y1 = [x0[s + 1] - x0[s] for s in (0, 2)]
            total[0] = total[0] + (y0[0] + y0[1])
            total[1] = total[1] + ((x1[0] + x1[1]) + (x1[2] + x1[3])) * mags[0]
            total[2] = total[2] + (y1[0] + y1[1]) * mags[1]
            total[3] = total[3] + (y0[1] - y0[0]) * mags[2]
        mine = lax.broadcasted_iota(jnp.int32, (16, 128), 0) == n
        near = [
            jnp.sum(jnp.where(mine, acc[:, 128 * q : 128 * q + 128], 0.0), 0, keepdims=True) for q in range(5)
        ]
        scale = 1.0 / FOUR_PI
        out_ref[0:1, at] = scale * (jnp.sum(pot, 0, keepdims=True) + near[0])
        for a in range(3):
            whole = jnp.sum(y[a] * total[0] - 0.5 * total[1 + a], 0, keepdims=True)
            out_ref[1 + a : 2 + a, at] = -scale * (whole + (xrel[a : a + 1, at] * near[1] - near[2 + a]))

    uexp0[...] = mm(dens, hot[0])

    def far_pair(i, carry):
        uexp1[...] = mm(dens, hot[2 * i + 1])
        for h in range(2):
            far_tile(4 * i + h, uexp0, slice(128 * h, 128 * h + 128))
        uexp0[...] = mm(dens, hot[jnp.minimum(2 * i + 2, 7)])
        for h in range(2):
            far_tile(4 * i + 2 + h, uexp1, slice(128 * h, 128 * h + 128))
        return carry

    lax.fori_loop(0, 4, far_pair, 0)
    if remote:
        pl.when(jnp.logical_and(there[0], box != 31))(halo[0].wait_send)
        pl.when(there[1])(halo[1].wait_send)
        pl.when(box == 31)(lent.wait_send)
        pl.when(box == 0)(passed.wait_send)

        @pl.when(early)
        def _():
            for copy in first[:3] + second + [third]:
                copy.wait_send()

        @pl.when(late)
        def _():
            for copy in first[3:]:
                copy.wait_send()


def run(remote, *args):
    vmem = pl.BlockSpec(memory_space=pltpu.VMEM)
    smem = pl.BlockSpec(memory_space=pltpu.SMEM)
    anys = pl.BlockSpec(memory_space=pl.ANY)
    constants = [jnp.asarray(value) for value in tables()]
    dma = pltpu.SemaphoreType.DMA
    return pl.pallas_call(
        functools.partial(kernel, remote),
        out_shape=jax.ShapeDtypeStruct((4, 2048), F32),
        in_specs=([] if remote else [smem, vmem, vmem]) + [anys] * 3 + [vmem] + [anys] * 12,
        out_specs=vmem,
        scratch_shapes=[
            pltpu.SMEM((512,), jnp.int32),
            pltpu.SMEM((64,), jnp.int32),
            pltpu.SMEM((64,), jnp.int32),
            pltpu.VMEM((1, 64), jnp.int32),
            pltpu.VMEM((1, 64), jnp.int32),
            pltpu.VMEM((3, 2048), F32),
            pltpu.VMEM((8, NPTS), F32),
            pltpu.VMEM((64, NPTS), F32),
            pltpu.VMEM((WID, NPTS), F32),
            pltpu.VMEM((WID, 2 * WID), BF16),
            pltpu.VMEM((WID, WID), BF16),
            pltpu.VMEM((WID, WID), BF16),
            pltpu.VMEM((4, BLK, 128), F32),
            dma((15,)),
            pltpu.VMEM((8, 1, NPTS), F32),
            pltpu.VMEM((7, 2, 1, NPTS), F32),
            pltpu.VMEM((8, 2, 1, NPTS), F32),
            pltpu.VMEM((3, 4, 1024), F32),
            pltpu.VMEM((1, NPTS), F32),
            pltpu.VMEM((1, NPTS), F32),
            dma((7,)),
            dma((7,)),
            dma((7,)),
            dma((7,)),
            dma((2,)),
            dma((2,)),
            dma((1,)),
            dma((1,)),
            pltpu.VMEM((4, 1024), F32),
            dma((2,)),
            dma((2,)),
            pltpu.VMEM((WID, 2 * WID), BF16),
            pltpu.VMEM((WID, 2 * WID), BF16),
            pltpu.VMEM((128, WID), F32),
            pltpu.VMEM((WID, 128), F32),
            pltpu.VMEM((WID, 128), F32),
            pltpu.VMEM((8, 128, 256), BF16),
            pltpu.VMEM((8, 2048), F32),
            pltpu.VMEM((32, 2048), F32),
            pltpu.VMEM((16, 32, 128), BF16),
            pltpu.VMEM((128, 1024), F32),
            pltpu.VMEM((24, 128, 128), BF16),
            pltpu.VMEM((24, 4, 128, 128), F32),
            pltpu.VMEM((512, 640), F32),
            pltpu.VMEM((16, 640), F32),
            pltpu.VMEM((WID, 256), F32),
            pltpu.VMEM((WID, 256), F32),
            pltpu.VMEM((UNROLL // 2, 128, 256), F32),
            pltpu.VMEM((UNROLL // 2, 128, 256), F32),
            pltpu.VMEM((16, WID, 128), F32),
            pltpu.VMEM((16, WID, 128), F32),
        ],
        compiler_params=pltpu.CompilerParams(
            vmem_limit_bytes=56 * 1024 * 1024, **(dict(collective_id=0, has_side_effects=True) if remote else {})
        ),
        name="downward",
    )(*args, *constants)


def per_device(
    coarse_dens, owner_slot, check_to_equiv, parent_own, leaf_own, leaf_counts, particles, panels, near_part,
    near_pan, near_count,
):
    return run(
        True, owner_slot, near_part, near_pan, near_count.reshape(1, 1), near_part.reshape(1, 64), leaf_counts, coarse_dens.T, panels,
        particles, parent_own.T, leaf_own.T, check_to_equiv,
    )


def solution(mesh):
    both = ("grp", "box")
    placed = (
        P(None, both), P(), P(), P(None, both), P(None, both), P(both, None), P(None, both), P(None, both), P(both),
        P(both), P(both),
    )
    return jax.shard_map(per_device, mesh=mesh, in_specs=placed, out_specs=P(None, both), check_vma=False)
```

```python
import functools
import math

import jax
import jax.numpy as jnp
import ml_dtypes
import numpy as np
from jax import lax
from jax.experimental import pallas as pl
from jax.experimental.pallas import tpu as pltpu
from jax.sharding import PartitionSpec as P

ORDER = 12
EQUIV_RADIUS = 2.95
CHECK_RADIUS = 1.05
SOFTEN_SQ = 0.0625
FOUR_PI = 4.0 * math.pi
MESH = pl.DeviceIdType.MESH

NPTS = 728
MAGS = 91
BLK = 96
WID = 8 * BLK
F32, BF16 = jnp.float32, jnp.bfloat16


def surface_points(edge_points):
    spacing = np.linspace(-1.0, 1.0, edge_points)
    lattice = np.stack(np.meshgrid(spacing, spacing, spacing, indexing="ij"), 0).reshape(3, -1)
    on_surface = np.max(np.abs(lattice), axis=0) > 0.999
    return lattice[:, on_surface].astype(np.float32)


def split2(value):
    hi = value.astype(ml_dtypes.bfloat16)
    lo = (value - hi.astype(np.float32)).astype(ml_dtypes.bfloat16)
    return hi, lo


@functools.lru_cache(maxsize=None)
def tables():
    points = surface_points(ORDER).astype(np.float64)
    grid = np.rint((points + 1.0) * (ORDER - 1) / 2.0).astype(int)
    index = {tuple(g): i for i, g in enumerate(grid.T)}
    half = ORDER // 2
    mags = [g for g in grid.T if min(g) >= half]
    order = np.full(WID, -1)
    for s in range(8):
        for m, g in enumerate(mags):
            key = tuple(g[a] if s >> a & 1 else ORDER - 1 - g[a] for a in range(3))
            order[BLK * s + m] = index[key]
    live = order >= 0
    placed = points[:, np.where(live, order, 0)]
    targets = -0.5 + 0.5 * CHECK_RADIUS * placed
    separation = targets[:, :, None] - EQUIV_RADIUS * placed[:, None, :]
    k0 = 1.0 / (FOUR_PI * np.sqrt(np.sum(separation * separation, 0)))
    k0 = np.where(live[:, None] & live[None, :], k0, 0.0).astype(np.float32)
    k_pair = np.concatenate(split2(k0), 1)
    perm = np.zeros((WID, WID), np.float32)
    perm[np.nonzero(live)[0], order[live]] = 1.0
    size = np.ones((3, BLK))
    size[:, :MAGS] = np.array([[points[a, index[tuple(g)]] for g in mags] for a in range(3)])
    rows = np.concatenate([2.0 * EQUIV_RADIUS * size, EQUIV_RADIUS**2 * np.sum(size * size, 0)[None]], 0)
    mag = np.broadcast_to(rows.astype(np.float32)[:, :, None], (4, BLK, 128)).copy()
    return k_pair, perm.astype(ml_dtypes.bfloat16), perm.T.copy().astype(ml_dtypes.bfloat16), mag


def pieces3(value):
    hi = value.astype(BF16).astype(F32)
    rest = value - hi
    mid = rest.astype(BF16).astype(F32)
    return hi, mid, (rest - mid).astype(BF16).astype(F32)


def mm(a, b):
    return jnp.dot(a, b, preferred_element_type=F32)


UNROLL = 8


def kernel(
    remote, *refs,
):
    if not remote:
        device_ref, coarse_in, win_in, *refs = refs
    (
        owner_hbm, part_hbm, pan_hbm, count_ref, tile_hbm, counts_hbm, coarse_hbm, panels_hbm, parts_hbm, pown_hbm, lown_hbm,
        m_hbm, k_hbm, perm_hbm, permt_hbm, mag_hbm, out_ref,
        owner_ref, part_s, pan_s, tile_ref, counts_ref, parts_ref, pown_ref, lown_ref, m_ref, k_ref, perm_ref, permt_ref, mag_ref, load_sem,
        line, picked, crossed, win, relay, got, send1, recv1, send2, recv2, send3, recv3, send4, recv4, extra, send5, recv5,
        m_half, m_pair, turn, pown, lown, hot, xrel, xf, xk, pf, pk, zb, slots, acc, uexp0, uexp1, sq0, sq1, inv_one, inv_cube,
    ) = refs
    if remote:
        grp, box = lax.axis_index("grp"), lax.axis_index("box")
        row, col = box // 8, box % 8
        me = grp * 64 + box
        early = box < 32
        late = box >= 32
        nxt, prv = lax.rem(me + 1, 512), lax.rem(me + 511, 512)
        cols = [row * 8 + lax.rem(col + r, 8) for r in range(1, 8)]
        along, side = row % 4, row // 4
        near_rows = [(side * 4 + lax.rem(along + r, 4)) * 8 + col for r in range(1, 4)]
        far_rows = [((1 - side) * 4 + lax.rem(along + r, 4)) * 8 + col for r in range(4)]
        rows = near_rows + far_rows
        beside = [(nxt // 64, nxt % 64), (prv // 64, prv % 64)]
        there = [me < 511, me > 0]
        turned_back = jnp.logical_and(col == 0, jnp.logical_or(box == 0, box > 32))
        greet = [
            jnp.logical_and(there[0], jnp.logical_or(col != 7, box <= 31)),
            jnp.logical_and(there[1], box != 32),
        ]
        hear = [jnp.logical_and(there[0], box != 31), jnp.logical_and(there[1], jnp.logical_not(turned_back))]
        answer = jnp.logical_and(there[1], turned_back)
        plain = jnp.logical_and(early, jnp.logical_and(box != 0, col < 4))
        barrier = pltpu.get_barrier_semaphore()

        @pl.when(early)
        def _():
            for other in near_rows + cols + far_rows:
                pl.semaphore_signal(barrier, inc=1, device_id=(grp, other), device_id_type=MESH)

        @pl.when(box == 0)
        def _():
            pl.semaphore_signal(barrier, inc=1, device_id=(grp, 31), device_id_type=MESH)

        @pl.when(box == 31)
        def _():
            pl.semaphore_signal(barrier, inc=1, device_id=(grp, 0), device_id_type=MESH)

        for r in range(2):

            @pl.when(greet[r])
            def _(r=r):
                pl.semaphore_signal(barrier, inc=1, device_id=beside[r], device_id_type=MESH)

        device = me
    else:
        row = 0
        device = device_ref[0]
    moves = {
        "coarse": (coarse_hbm, line.at[row]), "panels": (panels_hbm, win.at[1]), "owner": (owner_hbm, owner_ref),
        "counts": (counts_hbm, counts_ref), "parts": (parts_hbm, parts_ref), "part": (part_hbm, part_s),
        "pan": (pan_hbm, pan_s), "tile": (tile_hbm, tile_ref), "pown": (pown_hbm, pown_ref), "lown": (lown_hbm, lown_ref), "m": (m_hbm, m_ref.at[0:NPTS]),
        "permt": (permt_hbm, permt_ref), "perm": (perm_hbm, perm_ref), "k": (k_hbm, k_ref), "mag": (mag_hbm, mag_ref),
    }
    loads = {
        name: pltpu.make_async_copy(src, dst, load_sem.at[i]) for i, (name, (src, dst)) in enumerate(moves.items())
    }
    for load in loads.values():
        load.start()
    if remote:
        first = [
            pltpu.make_async_remote_copy(
                src_ref=coarse_hbm, dst_ref=line.at[row], send_sem=send1.at[r], recv_sem=recv1.at[r],
                device_id=(grp, rows[r]), device_id_type=MESH,
            )
            for r in range(7)
        ]
        second = [
            pltpu.make_async_remote_copy(
                src_ref=picked.at[r], dst_ref=crossed.at[col], send_sem=send2.at[r], recv_sem=recv2.at[r],
                device_id=(grp, cols[r]), device_id_type=MESH,
            )
            for r in range(7)
        ]
        third = pltpu.make_async_remote_copy(
            src_ref=relay, dst_ref=got, send_sem=send4.at[0], recv_sem=recv4.at[0],
            device_id=(grp, far_rows[0]), device_id_type=MESH,
        )
        lent = pltpu.make_async_remote_copy(
            src_ref=panels_hbm, dst_ref=extra, send_sem=send5.at[0], recv_sem=recv5.at[0],
            device_id=(grp, 0), device_id_type=MESH,
        )
        passed = pltpu.make_async_remote_copy(
            src_ref=extra, dst_ref=win.at[0], send_sem=send5.at[1], recv_sem=recv5.at[1],
            device_id=(grp, 32), device_id_type=MESH,
        )
        halo = [
            pltpu.make_async_remote_copy(
                src_ref=panels_hbm, dst_ref=win.at[2 * r], send_sem=send3.at[r], recv_sem=recv3.at[r],
                device_id=beside[r], device_id_type=MESH,
            )
            for r in range(2)
        ]

    lane = lax.broadcasted_iota(jnp.int32, (1, 128), 1)

    axis = lax.broadcasted_iota(jnp.int32, (4, 1), 0)
    shift = jnp.zeros((4, 1), jnp.int32)
    for b in range(3):
        bit = jnp.bitwise_and(jnp.right_shift(device, 3 * b + axis), 1)
        shift = shift + jnp.left_shift(bit, b)
    centre = jnp.where(axis < 3, (8 * shift + 4).astype(F32), 0.0)

    def panel_part(s):
        raw = win[s] - centre
        z = raw[0:3]
        hi, mid, low = pieces3(z)
        for r, piece in enumerate((hi, hi, mid, hi, low, mid)):
            pf[3 * r : 3 * r + 3, :] = -2.0 * piece
        pf[18:21, :] = jnp.ones((3, 1024), F32)
        for r, piece in enumerate(pieces3(jnp.sum(z * z, 0, keepdims=True) + SOFTEN_SQ)):
            pf[21 + r : 22 + r, :] = piece
        pf[24:28, :] = raw

        for t in range(8):
            turned = pf[:, 128 * t : 128 * t + 128].T
            operand = turned[:, 0:32].astype(BF16)
            pk[8 * s + t] = jnp.zeros((128, 128), BF16)
            pk[8 * s + t, :, 0:32] = operand
            pk[8 * s + t, :, 64:96] = operand
            for a in range(4):
                zb[8 * s + t, a] = jnp.broadcast_to(turned[:, 24 + a : 25 + a], (128, 128))

    def prepare():
        loads["counts"].wait()
        counts = counts_ref[...].astype(F32)
        g_row = lax.broadcasted_iota(jnp.int32, (64, 64), 0)
        g_col = lax.broadcasted_iota(jnp.int32, (64, 64), 1)
        upto = jnp.sum(jnp.where(g_col <= g_row, counts, 0.0), 1, keepdims=True)
        before = jnp.sum(jnp.where(g_col < g_row, counts, 0.0), 1, keepdims=True)
        leaf = lax.broadcasted_iota(jnp.int32, (64, 1), 0)
        local = []
        for a in range(3):
            c = jnp.bitwise_and(jnp.right_shift(leaf, a), 1) + 2 * jnp.bitwise_and(jnp.right_shift(leaf, 3 + a), 1)
            local.append((2 * c - 3).astype(F32))
        loads["parts"].wait()
        for n in range(16):
            index = (lax.broadcasted_iota(jnp.int32, (1, 128), 1) + 128 * n).astype(F32)
            inside = jnp.where((index >= before) & (index < upto), 1.0, 0.0)
            side = slice(128 * (n % 2), 128 * (n % 2) + 128)
            hot[n // 2, 0:64, side] = inside.astype(BF16)
            hot[n // 2, 64:128, side] = inside.astype(BF16)
            for a in range(3):
                centre = jnp.sum(inside * local[a], 0, keepdims=True)
                xrel[a : a + 1, 128 * n : 128 * n + 128] = parts_ref[a : a + 1, 128 * n : 128 * n + 128] + centre

        xf[...] = jnp.zeros_like(xf)
        x = xrel[0:3, :]
        hi, mid, low = pieces3(x)
        for r, piece in enumerate((hi, mid, hi, low, hi, mid)):
            xf[3 * r : 3 * r + 3, :] = piece
        for r, piece in enumerate(pieces3(jnp.sum(x * x, 0, keepdims=True))):
            xf[18 + r : 19 + r, :] = piece
        xf[21:24, :] = jnp.ones((3, 2048), F32)
        for n in range(16):
            xk[n] = xf[:, 128 * n : 128 * n + 128].astype(BF16)
        pf[28:128, :] = jnp.zeros((100, 1024), F32)
        loads["panels"].wait()
        panel_part(1)

        loads["perm"].wait()

        def placed_own():
            value = turn[...]
            hi = value.astype(BF16).astype(F32)
            both = jnp.where(lax.broadcasted_iota(jnp.int32, (128, 1), 0) < 64, hi, value - hi).astype(BF16)
            product = lax.dot_general(perm_ref[...], both, (((1,), (1,)), ((), ())), preferred_element_type=F32)
            return product + pltpu.roll(product, 64, 1)

        turn[:, 640:WID] = jnp.zeros((128, 128), F32)
        loads["pown"].wait()
        for k in range(8):
            value = jnp.broadcast_to(pown_ref[k : k + 1, :], (8, NPTS))
            turn[8 * k : 8 * k + 8, 0:NPTS] = value
            turn[64 + 8 * k : 72 + 8 * k, 0:NPTS] = value
        pown[...] = placed_own()
        loads["lown"].wait()
        turn[0:64, 0:NPTS] = lown_ref[...]
        turn[64:128, 0:NPTS] = lown_ref[...]
        lown[...] = placed_own()


    def prepare_m():
        m_ref[NPTS:WID] = jnp.zeros((WID - NPTS, NPTS), F32)
        loads["m"].wait()
        loads["permt"].wait()
        m_half[:, 640:WID] = jnp.zeros((WID, 128), BF16)
        m_half[:, WID + 640 : 2 * WID] = jnp.zeros((WID, 128), BF16)

        def m_split(r, carry):
            at = pl.ds(pl.multiple_of(r * 64, 64), 64)
            value = m_ref[at, :]
            hi = value.astype(BF16)
            m_half[at, 0:NPTS] = hi
            m_half[at, WID : WID + NPTS] = (value - hi.astype(F32)).astype(BF16)
            return carry

        lax.fori_loop(0, 12, m_split, 0)

        def m_columns(r, carry):
            at = pl.ds(pl.multiple_of(r * 256, 256), 256)
            for side in (slice(0, WID), slice(WID, 2 * WID)):
                m_half[at, side] = mm(m_half[at, side], permt_ref[...]).astype(BF16)
            return carry

        lax.fori_loop(0, 3, m_columns, 0)

        def m_rows(r, carry):
            at = pl.ds(pl.multiple_of(r * 256, 256), 256)
            m_pair[:, at] = mm(perm_ref[...], m_half[:, at]).astype(BF16)
            return carry

        lax.fori_loop(0, 6, m_rows, 0)


    def prepare_far():
        loads["mag"].wait()

        def distances(n, carry):
            at = pl.ds(pl.multiple_of(n * 128, 128), 128)
            y = [jnp.broadcast_to(parts_ref[a : a + 1, at], (8, 128)) for a in range(3)]
            y2 = y[0] * y[0] + y[1] * y[1] + y[2] * y[2]
            for v in range(BLK // 8):
                band = slice(8 * v, 8 * v + 8)
                part = [y2 + mag_ref[3, band]]
                for a in range(3):
                    step = y[a] * mag_ref[a, band]
                    part = [q + step for q in part] + [q - step for q in part]
                for s in range(8):
                    inv = lax.rsqrt(part[s])
                    inv_one[n, BLK * s + 8 * v : BLK * s + 8 * v + 8] = inv
                    inv_cube[n, BLK * s + 8 * v : BLK * s + 8 * v + 8] = inv * (inv * inv)
            return carry

        lax.fori_loop(0, 16, distances, 0)

    def window_next():
        if remote:
            pl.when(there[0])(halo[1].wait_recv)

            @pl.when(jnp.logical_not(there[0]))
            def _():
                win[2] = jnp.zeros((4, 1024), F32)

        panel_part(2)

    def window_previous():
        if remote:
            pl.when(box == 32)(passed.wait_recv)
            pl.when(jnp.logical_and(there[1], jnp.logical_not(jnp.logical_or(answer, box == 32))))(halo[0].wait_recv)

            @pl.when(jnp.logical_not(there[1]))
            def _():
                win[0] = jnp.zeros((4, 1024), F32)

        panel_part(0)

    def window():
        window_next()
        window_previous()

    if remote:
        pl.when(early)(prepare)
        heard = 4 + 6 * early.astype(jnp.int32) + hear[0].astype(jnp.int32) + hear[1].astype(jnp.int32)
        heard = heard + jnp.logical_or(box == 0, box == 31).astype(jnp.int32)
        pl.semaphore_wait(barrier, heard)
        pl.when(box == 31)(lent.start)

        @pl.when(late)
        def _():
            for copy in first[3:]:
                copy.start()

        @pl.when(early)
        def _():
            for copy in first[:3]:
                copy.start()

        for r in range(2):
            pl.when(hear[r])(halo[r].start)
        pl.when(late)(prepare)
        prepare_m()

        @pl.when(jnp.logical_and(answer, late))
        def _():
            halo[0].wait_recv()
            halo[1].start()

        pl.when(jnp.logical_or(late, col < 4))(prepare_far)
        loads["owner"].wait()
        loads["coarse"].wait()
        pl.when(plain)(window)

        @pl.when(early)
        def _():
            for copy in first:
                copy.wait_recv()

            @pl.when(box == 0)
            def _():
                lent.wait_recv()
                passed.start()

            for r in range(8):
                for h in range(2):
                    whose = (row + 4 * h) * 8 + lax.rem(col + r, 8)
                    want = jnp.bitwise_and(jnp.right_shift(owner_ref[grp * 64 + whose], 3), 7)
                    if r == 0:
                        crossed[col, h] = line[want]
                    else:
                        picked[r - 1, h] = line[want]
            for copy in second:
                copy.start()

        pl.when(jnp.logical_not(plain))(window_next)

        @pl.when(jnp.logical_and(answer, early))
        def _():
            halo[0].wait_recv()
            halo[1].start()

        pl.when(jnp.logical_not(plain))(window_previous)
    else:
        prepare()
        win[0] = win_in[0]
        win[2] = win_in[2]
        loads["owner"].wait()
        loads["coarse"].wait()
        prepare_m()
        prepare_far()
        window()

    loads["part"].wait()
    loads["pan"].wait()
    left = lax.broadcasted_iota(jnp.int32, (128, 128), 1) < 64
    blank = jnp.zeros((32, 128), BF16)

    def near_squares(i, into):
        for u in range(UNROLL // 2):
            t = i * UNROLL + 2 * u
            panel = jnp.where(left, pk[pan_s[t]], pk[pan_s[t + 1]])[:, 0:96]
            one, two = xk[part_s[t]], xk[part_s[t + 1]]
            part = jnp.concatenate(
                [jnp.concatenate([one, blank, blank], 0), jnp.concatenate([blank, blank, two], 0)], 1
            )
            into[u] = mm(panel, part)

    def near_sums(i, squares):
        for u in range(UNROLL):
            t = i * UNROLL + u
            tile = pan_s[t]
            side = slice(128 * (u % 2), 128 * (u % 2) + 128)
            sums = [jnp.zeros((8, 128), F32)] * 5
            for v in range(16):
                at = slice(8 * v, 8 * v + 8)
                inv = lax.rsqrt(squares[u // 2, at, side])
                w = zb[tile, 3, at] * inv
                w3 = w * (inv * inv)
                sums[0] = sums[0] + w
                sums[1] = sums[1] + w3
                for a in range(3):
                    sums[2 + a] = sums[2 + a] + w3 * zb[tile, a, at]
            at = pl.ds(pl.multiple_of(t * 8, 8), 8)
            for q in range(5):
                slots[at, 128 * q : 128 * q + 128] = sums[q]

    near_squares(0, sq0)
    steps = 64 // UNROLL

    def near_slots(i, carry):
        near_squares(2 * i + 1, sq1)
        near_sums(2 * i, sq0)
        near_squares(jnp.minimum(2 * i + 2, steps - 1), sq0)
        near_sums(2 * i + 1, sq1)
        return carry

    lax.fori_loop(0, steps // 2, near_slots, 0)
    if remote:
        pl.when(jnp.logical_and(early, col >= 4))(prepare_far)
    loads["tile"].wait()
    slot = lax.broadcasted_iota(jnp.int32, (1, 64), 1)
    live = jnp.where(slot < count_ref[...], tile_ref[...], 31).astype(F32)
    e_row = lax.broadcasted_iota(jnp.int32, (64, 512), 0)
    e_col = lax.broadcasted_iota(jnp.int32, (64, 512), 1)
    spread8 = jnp.where(jnp.right_shift(e_col, 3) == e_row, 1.0, 0.0).astype(BF16)
    target = mm(jnp.broadcast_to(live, (16, 64)).astype(BF16), spread8)
    n_row = lax.broadcasted_iota(jnp.int32, (16, 512), 0).astype(F32)
    choose = jnp.where(target == n_row, 1.0, 0.0).astype(BF16)
    hi, mid, low = pieces3(slots[...])
    acc[...] = mm(choose, hi.astype(BF16)) + (mm(choose, mid.astype(BF16)) + mm(choose, low.astype(BF16)))

    low_half = lane < 64
    column = jnp.bitwise_and(lane, 63)

    def swapped(value, octant):
        blocks = [value[BLK * s : BLK * s + BLK] for s in range(8)]
        for b in range(3):
            mask = jnp.bitwise_and(jnp.right_shift(octant, b), 1) == 1
            blocks = [jnp.where(mask, blocks[s ^ (1 << b)], blocks[s]) for s in range(8)]
        return jnp.concatenate(blocks, 0)

    def pieces(value):
        hi = value.astype(BF16).astype(F32)
        return jnp.where(low_half, hi, value - hi).astype(BF16)

    def both(pair_ref, x2):
        product = mm(pair_ref[...], jnp.concatenate([x2, x2], 0))
        return product + pltpu.roll(product, 64, 1)

    def level(x2, octant, own):
        checks = swapped(pieces(both(k_ref, swapped(x2, octant))), octant)
        return both(m_pair, checks) + own

    loads["k"].wait()
    if remote:

        @pl.when(early)
        def _():
            for copy in second:
                copy.wait_recv()
            got[...] = crossed[jnp.bitwise_and(owner_ref[me], 7), 0]
            relay[...] = crossed[jnp.bitwise_and(owner_ref[me + 32], 7), 1]
            third.start()

        pl.when(late)(third.wait_recv)
        coarse = got[...]
    else:
        coarse = coarse_in[...]
    half = lax.broadcasted_iota(jnp.int32, (128, 1), 0) < 64
    hi = coarse.astype(BF16).astype(F32)
    turn[:, 0:NPTS] = jnp.where(half, hi, coarse - hi)
    spread = turn[...].astype(BF16)
    start = lax.dot_general(perm_ref[...], spread, (((1,), (1,)), ((), ())), preferred_element_type=F32)
    parents = level(start.astype(BF16), jnp.right_shift(column, 3), pown[...])
    leaves = level(pieces(parents), jnp.bitwise_and(column, 7), lown[...])
    dens = pieces(leaves)

    def far_tile(n, dense, side):
        at = pl.ds(pl.multiple_of(n * 128, 128), 128)
        y = [jnp.broadcast_to(parts_ref[a : a + 1, at], (8, 128)) for a in range(3)]
        pot = jnp.zeros((8, 128), F32)
        total = [jnp.zeros((8, 128), F32)] * 4
        for v in range(BLK // 8):
            band = slice(8 * v, 8 * v + 8)
            mags = [mag_ref[a, band] for a in range(3)]
            w3 = []
            for s in range(8):
                at8 = slice(BLK * s + 8 * v, BLK * s + 8 * v + 8)
                u = dense[at8, side]
                pot = pot + u * inv_one[n, at8]
                w3.append(u * inv_cube[n, at8])
            x0 = [w3[s] + w3[s + 1] for s in (0, 2, 4, 6)]
            x1 = [w3[s + 1] - w3[s] for s in (0, 2, 4, 6)]
            y0 = [x0[s] + x0[s + 1] for s in (0, 2)]
            y1 = [x0[s + 1] - x0[s] for s in (0, 2)]
            total[0] = total[0] + (y0[0] + y0[1])
            total[1] = total[1] + ((x1[0] + x1[1]) + (x1[2] + x1[3])) * mags[0]
            total[2] = total[2] + (y1[0] + y1[1]) * mags[1]
            total[3] = total[3] + (y0[1] - y0[0]) * mags[2]
        mine = lax.broadcasted_iota(jnp.int32, (16, 128), 0) == n
        near = [
            jnp.sum(jnp.where(mine, acc[:, 128 * q : 128 * q + 128], 0.0), 0, keepdims=True) for q in range(5)
        ]
        scale = 1.0 / FOUR_PI
        out_ref[0:1, at] = scale * (jnp.sum(pot, 0, keepdims=True) + near[0])
        for a in range(3):
            whole = jnp.sum(y[a] * total[0] - 0.5 * total[1 + a], 0, keepdims=True)
            out_ref[1 + a : 2 + a, at] = -scale * (whole + (xrel[a : a + 1, at] * near[1] - near[2 + a]))

    uexp0[...] = mm(dens, hot[0])

    def far_pair(i, carry):
        uexp1[...] = mm(dens, hot[2 * i + 1])
        for h in range(2):
            far_tile(4 * i + h, uexp0, slice(128 * h, 128 * h + 128))
        uexp0[...] = mm(dens, hot[jnp.minimum(2 * i + 2, 7)])
        for h in range(2):
            far_tile(4 * i + 2 + h, uexp1, slice(128 * h, 128 * h + 128))
        return carry

    lax.fori_loop(0, 4, far_pair, 0)
    if remote:
        pl.when(jnp.logical_and(there[0], box != 31))(halo[0].wait_send)
        pl.when(there[1])(halo[1].wait_send)
        pl.when(box == 31)(lent.wait_send)
        pl.when(box == 0)(passed.wait_send)

        @pl.when(early)
        def _():
            for copy in first[:3] + second + [third]:
                copy.wait_send()

        @pl.when(late)
        def _():
            for copy in first[3:]:
                copy.wait_send()


def run(remote, *args):
    vmem = pl.BlockSpec(memory_space=pltpu.VMEM)
    smem = pl.BlockSpec(memory_space=pltpu.SMEM)
    anys = pl.BlockSpec(memory_space=pl.ANY)
    constants = [jnp.asarray(value) for value in tables()]
    dma = pltpu.SemaphoreType.DMA
    return pl.pallas_call(
        functools.partial(kernel, remote),
        out_shape=jax.ShapeDtypeStruct((4, 2048), F32),
        in_specs=([] if remote else [smem, vmem, vmem]) + [anys] * 3 + [vmem] + [anys] * 12,
        out_specs=vmem,
        scratch_shapes=[
            pltpu.SMEM((512,), jnp.int32),
            pltpu.SMEM((64,), jnp.int32),
            pltpu.SMEM((64,), jnp.int32),
            pltpu.VMEM((1, 64), jnp.int32),
            pltpu.VMEM((1, 64), jnp.int32),
            pltpu.VMEM((3, 2048), F32),
            pltpu.VMEM((8, NPTS), F32),
            pltpu.VMEM((64, NPTS), F32),
            pltpu.VMEM((WID, NPTS), F32),
            pltpu.VMEM((WID, 2 * WID), BF16),
            pltpu.VMEM((WID, WID), BF16),
            pltpu.VMEM((WID, WID), BF16),
            pltpu.VMEM((4, BLK, 128), F32),
            dma((15,)),
            pltpu.VMEM((8, 1, NPTS), F32),
            pltpu.VMEM((7, 2, 1, NPTS), F32),
            pltpu.VMEM((8, 2, 1, NPTS), F32),
            pltpu.VMEM((3, 4, 1024), F32),
            pltpu.VMEM((1, NPTS), F32),
            pltpu.VMEM((1, NPTS), F32),
            dma((7,)),
            dma((7,)),
            dma((7,)),
            dma((7,)),
            dma((2,)),
            dma((2,)),
            dma((1,)),
            dma((1,)),
            pltpu.VMEM((4, 1024), F32),
            dma((2,)),
            dma((2,)),
            pltpu.VMEM((WID, 2 * WID), BF16),
            pltpu.VMEM((WID, 2 * WID), BF16),
            pltpu.VMEM((128, WID), F32),
            pltpu.VMEM((WID, 128), F32),
            pltpu.VMEM((WID, 128), F32),
            pltpu.VMEM((8, 128, 256), BF16),
            pltpu.VMEM((8, 2048), F32),
            pltpu.VMEM((32, 2048), F32),
            pltpu.VMEM((16, 32, 128), BF16),
            pltpu.VMEM((128, 1024), F32),
            pltpu.VMEM((24, 128, 128), BF16),
            pltpu.VMEM((24, 4, 128, 128), F32),
            pltpu.VMEM((512, 640), F32),
            pltpu.VMEM((16, 640), F32),
            pltpu.VMEM((WID, 256), F32),
            pltpu.VMEM((WID, 256), F32),
            pltpu.VMEM((UNROLL // 2, 128, 256), F32),
            pltpu.VMEM((UNROLL // 2, 128, 256), F32),
            pltpu.VMEM((16, WID, 128), F32),
            pltpu.VMEM((16, WID, 128), F32),
        ],
        compiler_params=pltpu.CompilerParams(
            vmem_limit_bytes=56 * 1024 * 1024, **(dict(collective_id=0, has_side_effects=True) if remote else {})
        ),
        name="downward",
    )(*args, *constants)


def per_device(
    coarse_dens, owner_slot, check_to_equiv, parent_own, leaf_own, leaf_counts, particles, panels, near_part,
    near_pan, near_count,
):
    return run(
        True, owner_slot, near_part, near_pan, near_count.reshape(1, 1), near_part.reshape(1, 64), leaf_counts, coarse_dens.T, panels,
        particles, parent_own.T, leaf_own.T, check_to_equiv,
    )


def solution(mesh):
    both = ("grp", "box")
    placed = (
        P(None, both), P(), P(), P(None, both), P(None, both), P(both, None), P(None, both), P(None, both), P(both),
        P(both), P(both),
    )
    return jax.shard_map(per_device, mesh=mesh, in_specs=placed, out_specs=P(None, both), check_vma=False)
```
